32 devices in a mesh: groups: 2 (over x), tile: 16 (over z, y, core).
Axes of the slice: x: 2, y: 2, z: 4, core: 2. Of those that a mesh axis runs over, the one named last changes fastest.
Arguments:
- walkers: bfloat16 [32, 512, 256], P(('groups', 'tile')), parts along dimension 0, may hold values from -6 to 6
- green_factor: bfloat16 [32, 512, 256], P(('groups', 'tile')), parts along dimension 0, may hold values from -6 to 6
- trial: bfloat16 [512, 256], replicated, may hold values from -0.375 to 0.375
- chol: bfloat16 [496, 2048, 256], P('tile'), may hold values from -0.01171875 to 0.01171875
- pattern: int32 [256], replicated, may hold values from 0 to 1023, as said below
- owner_counts: int32 [16], replicated, may hold values from 1 to 31, as said below
- chol_group: int32 [2048], replicated, may hold values from 0 to 3
- group_weight: float32 [4], replicated, may hold values from 0.5 to 2
- aux: int32 [32, 2048], P('groups'), parts along dimension 0, may hold values from -524288 to 524287
Outputs:
- advanced: bfloat16 [32, 512, 256], P(('groups', 'tile')), parts along dimension 0
- log_weight: float32 [32], P(('groups', 'tile')), parts along dimension 0
The draws below stay inside these ranges and needn't reach their ends.
There are 2 independent parts, one for each index of `groups`. The reference program is written for one: setup_inputs(seed, part) draws one part's arguments, and reference() takes and returns one part's arrays. A program takes and returns all parts, laid end to end along the dimension named above; an argument that names none is the same for every part. Nothing has to cross between parts.
Inputs may be any that keep to these rules, and one draw needn't show every extreme that they name: `pattern`: values are distinct. Owners d and d + 8 together hold 32 tiles; slots of owner d past owner_counts[d] hold no tile.
All inputs are finite; a program needn't handle non-finite values.
Results may differ from the reference program's by a relative error of at most 0.009.
Values may be sent and summed in bfloat16 or wider, within the bound.
A program may use at most 128 MiB of HBM per device.

```python
import math
import jax
import jax.numpy as jnp
from jax import lax

M = 512
NE = 256
NCHOL = 2048
NGRP = 4
NBLK = 32
BS2 = 256
NT = 256
CAP = 31
W = 16
N_TILE = 16


def draw_pattern(key, part):
    pair_count = NBLK * NBLK
    middle = jax.random.permutation(jax.random.fold_in(key, 11), pair_count - 2) + 1
    chosen = jnp.concatenate([jnp.array([0, pair_count - 1], jnp.int32), middle[:NT - 2].astype(jnp.int32)])
    shuffle = jax.random.permutation(jax.random.fold_in(key, 12), NT)
    return chosen[shuffle].astype(jnp.int32)


def draw_owner_counts(key, part):
    half_axis = N_TILE // 2
    per_device = NT // N_TILE
    first_half = jax.random.randint(jax.random.fold_in(key, 21), (half_axis,), 1, 2 * per_device, dtype=jnp.int32)
    heavy_slot = jax.random.randint(jax.random.fold_in(key, 22), (), 0, half_axis, dtype=jnp.int32)
    first_half = jnp.where(jnp.arange(half_axis, dtype=jnp.int32) == heavy_slot, 2 * per_device - 1, first_half)
    flipped = jax.random.randint(jax.random.fold_in(key, 23), (half_axis,), 0, 2, dtype=jnp.int32)
    lower = jnp.where(flipped == 1, 2 * per_device - first_half, first_half)
    return jnp.concatenate([lower, 2 * per_device - lower]).astype(jnp.int32)


def set_ends(entries, own_key, least, largest):
    spot = [jax.random.randint(jax.random.fold_in(own_key, axis), (), 0, length) for axis, length in enumerate(entries.shape)]
    longest = entries.shape.index(max(entries.shape))
    next_to = spot[:longest] + [(spot[longest] + 1) % entries.shape[longest]] + spot[longest + 1:]
    return entries.at[tuple(spot)].set(least).at[tuple(next_to)].set(largest)


def level_of(own_key, dims, pieces, smallest, largest):
    gain = 1.0
    for position, parts in pieces:
        draws = jax.random.uniform(jax.random.fold_in(jax.random.fold_in(own_key, 6), position), (parts,), jnp.float32, smallest / len(pieces), largest / len(pieces))
        gain = gain * jnp.repeat(jnp.exp(draws), dims[position] // parts).reshape((-1,) + (1,) * (len(dims) - 1 - position))
    return gain


def scatter_about(key, dims, deviation, reach, pieces=(), kind=jnp.bfloat16):
    values = deviation * jax.random.normal(key, dims, jnp.float32)
    if pieces:
        values = values * level_of(key, dims, pieces, -0.22, 0.18)
    return jnp.clip(values, -reach, reach).astype(kind)


def setup_inputs(seed: int = 0, part: int = 0) -> dict:
    key_list = jax.random.split(jax.random.key(seed), 10)
    own_keys = jax.random.split(jax.random.fold_in(key_list[9], part), 10)
    walkers = scatter_about(own_keys[0], (W, M, NE), 1.0, 6.0, ((0, 16),))
    green_factor = scatter_about(own_keys[1], (W, M, NE), 1.0, 6.0, ((0, 16),))
    trial = scatter_about(key_list[2], (M, NE), NE ** -0.5, 0.375)
    chol = scatter_about(key_list[3], (N_TILE * CAP, NCHOL, BS2), (NCHOL * M // 4) ** -0.5, 0.01171875, ((0, 16),))
    pattern = draw_pattern(jax.random.fold_in(key_list[9], 71), part)
    owner_counts = draw_owner_counts(jax.random.fold_in(key_list[9], 71), part)
    chol_group = set_ends(jax.random.randint(key_list[6], (NCHOL,), 0, NGRP), jax.random.fold_in(key_list[6], 1), 0, NGRP - 1).astype(jnp.int32)
    group_weight = jnp.clip(jnp.exp(jax.random.uniform(key_list[7], (NGRP,), jnp.float32, math.log(0.5), math.log(2.0))), 0.5, 2.0)
    aux = set_ends(jax.random.randint(own_keys[8], (W, NCHOL), -524288, 524288), jax.random.fold_in(own_keys[8], 1), -524288, 524287).astype(jnp.int32)
    return {"walkers": walkers, "green_factor": green_factor, "trial": trial, "chol": chol, "pattern": pattern, "owner_counts": owner_counts, "chol_group": chol_group, "group_weight": group_weight, "aux": aux}


def tile_slots(owner_counts):
    offsets = jnp.cumsum(owner_counts) - owner_counts
    tile_ids = jnp.arange(NT, dtype=jnp.int32)
    tile_ends = offsets + owner_counts
    owner_of = jnp.sum((tile_ids[:, None] >= tile_ends[None, :]).astype(jnp.int32), axis=1).astype(jnp.int32)
    return (owner_of * CAP + tile_ids - offsets[owner_of]).astype(jnp.int32)


def reference(walkers, green_factor, trial, chol, pattern, owner_counts, chol_group, group_weight, aux):
    block_side = M // NBLK
    row_blocks = (pattern // NBLK).astype(jnp.int32)
    col_blocks = (pattern % NBLK).astype(jnp.int32)
    chol_tiles = chol[tile_slots(owner_counts)]

    def green_tiles(factor_rows):
        green_full = jnp.dot(factor_rows, trial.T, preferred_element_type=jnp.float32).astype(jnp.bfloat16)
        blocks = green_full.reshape(NBLK, block_side, NBLK, block_side)
        return blocks[row_blocks, :, col_blocks, :].reshape(NT, block_side * block_side)

    green_all = lax.map(green_tiles, green_factor)
    force_bias = jnp.einsum("wte,tge->wg", green_all.astype(jnp.float32), chol_tiles.astype(jnp.float32))
    sampled = aux.astype(jnp.float32) * (1.0 / 262144.0)
    log_weight = jnp.sum(sampled * force_bias - 0.5 * force_bias * force_bias, axis=1)
    column_weight = group_weight[chol_group]
    fields = (column_weight[None, :] * (sampled - force_bias)).astype(jnp.bfloat16)
    potential = jnp.einsum("wg,tge->wte", fields.astype(jnp.float32), chol_tiles.astype(jnp.float32)).astype(jnp.bfloat16)

    def propagate(pair_args):
        walker, pot_tiles = pair_args
        tile_mats = pot_tiles.reshape(NT, block_side, block_side).astype(jnp.float32)
        taylor_term = walker
        running = walker.astype(jnp.float32)
        for degree in range(1, 5):
            gathered = taylor_term.reshape(NBLK, block_side, NE)[col_blocks].astype(jnp.float32)
            product = jnp.einsum("tpq,tqe->tpe", tile_mats, gathered)
            summed = jax.ops.segment_sum(product, row_blocks, num_segments=NBLK).reshape(M, NE)
            taylor_term = (summed / degree).astype(jnp.bfloat16)
            running = running + taylor_term.astype(jnp.float32)
        return running.astype(jnp.bfloat16)

    advanced = lax.map(propagate, (walkers, potential))
    return advanced, log_weight
```

```python
import functools

import jax
import jax.numpy as jnp
from jax import lax
from jax.experimental import pallas as pl
from jax.experimental.pallas import tpu as pltpu
from jax.sharding import PartitionSpec as P

NBLK = 32
BF = jnp.bfloat16
F32 = jnp.float32
NT_DIMS = (((1,), (1,)), ((), ()))


def quot(x, k):
    if k & (k - 1) == 0:
        return lax.shift_right_logical(x, jnp.int32(k.bit_length() - 1))
    return lax.div(x, jnp.int32(k))


def mod(x, k):
    if k & (k - 1) == 0:
        return lax.bitwise_and(x, jnp.int32(k - 1))
    return lax.rem(x, jnp.int32(k))


def iota(shape, dim):
    return lax.broadcasted_iota(jnp.int32, shape, dim)


def hot(cond):
    return jnp.where(cond, 1.0, 0.0).astype(BF)


def dot(a, b):
    return jnp.dot(a, b, preferred_element_type=F32)


def swap_matrix(outer, inner):
    size = outer * inner
    row = iota((size, size), 0)
    col = iota((size, size), 1)
    return hot(col == mod(row, inner) * outer + quot(row, inner))


def kernel(
    n, cap, slots, gstep,
    walk_ref, factor_ref, trial_ref, chol_ref, pattern_ref, counts_ref, cgroup_ref, gweight_ref,
    aux_ref,
    adv_ref, lw_ref,
    chol_v, perm_g, green_v, sent, got, tiles_v, part, part_got, field_own, field_got, field_all,
    logw_own, logw_got, pot_v, back, back_got, v_mat,
    chol_sem, a_send, a_recv, r_send, r_recv, f_send, f_recv, l_send, l_recv, b_send, b_recv,
):
    me = lax.axis_index("tile")
    orbitals, electrons = walk_ref.shape[1], walk_ref.shape[2]
    nchol, entries = chol_ref.shape[1], chol_ref.shape[2]
    ntile = pattern_ref.shape[1]
    wall = aux_ref.shape[0]
    side = orbitals // NBLK
    width = nchol // n
    rows = n * slots

    def send(src, dst, ssem, rsem, dev):
        return pltpu.make_async_remote_copy(
            src_ref=src, dst_ref=dst, send_sem=ssem, recv_sem=rsem,
            device_id={"tile": dev}, device_id_type=pl.DeviceIdType.MESH,
        )

    barrier = pltpu.get_barrier_semaphore()
    for off in range(1, n):
        pl.semaphore_signal(
            barrier, inc=1, device_id={"tile": lax.rem(me + off, n)},
            device_id_type=pl.DeviceIdType.MESH,
        )
    chol_copies = []
    for c in range(nchol // gstep):
        span = pl.ds(c * gstep, gstep)
        chol_copies.append(
            pltpu.make_async_copy(chol_ref.at[:, span, :], chol_v.at[:, span, :], chol_sem.at[c])
        )
        chol_copies[-1].start()

    perm = swap_matrix(side, NBLK)
    factor = dot(perm, factor_ref[0]).astype(BF)
    green_v[...] = lax.dot_general(
        factor, trial_ref[...], NT_DIMS, preferred_element_type=F32
    ).astype(BF)

    pat_row = pattern_ref[...]
    pat_col = jnp.transpose(jnp.broadcast_to(pat_row, (128, ntile)))[:, :1]
    row_pick = hot(quot(pat_col, NBLK) == iota((ntile, NBLK), 1))
    row_put = hot(quot(pat_row, NBLK) == iota((NBLK, ntile), 0))
    col_mask = hot(mod(pat_col, NBLK) == quot(iota((ntile, orbitals), 1), side))
    fold = hot(mod(iota((orbitals, entries), 0), side) == mod(iota((orbitals, entries), 1), side))
    entry_row = quot(iota((ntile, entries), 1), side)

    def pick(p, total):
        block = green_v[pl.ds(pl.multiple_of(p * NBLK, NBLK), NBLK), :]
        chosen = dot(row_pick, block).astype(BF) * col_mask
        return jnp.where(entry_row == p, dot(chosen, fold), total)

    green_t = lax.fori_loop(0, side, pick, jnp.zeros((ntile, entries), F32), unroll=True).astype(BF)

    first = jnp.int32(0)
    lane_tile = jnp.full((1, rows), -1, jnp.int32)
    lane = iota((1, rows), 1)
    for d in range(n):
        held = counts_ref[d]
        slot = iota((slots, ntile), 0)
        own = hot((iota((slots, ntile), 1) == slot + first) & (slot < held))
        sent[d] = dot(own, green_t).astype(BF)
        lane_slot = lane - d * slots
        live = (lane_slot >= 0) & (lane_slot < held)
        lane_tile = jnp.where(live, lane_slot + first, lane_tile)
        first = first + held

    pl.semaphore_wait(barrier, n - 1)
    a_copies = []
    for off in range(1, n):
        dst = lax.rem(me + off, n)
        a_copies.append(send(sent.at[dst], got.at[me], a_send.at[off], a_recv.at[off], dst))
        a_copies[-1].start()
    got[me] = sent[me]
    perm_g[...] = swap_matrix(slots, wall)
    for copy in a_copies:
        copy.wait_recv()
    tiles_v[...] = dot(perm_g[...], got[...].reshape(rows, entries)).astype(BF).reshape(
        slots, wall, entries
    )

    r_copies = []
    for c in range(nchol // gstep):
        chol_copies[c].wait()

        def add(j, total):
            return total + lax.dot_general(
                tiles_v[j], chol_v[j, c * gstep : (c + 1) * gstep, :], NT_DIMS,
                preferred_element_type=F32,
            )

        bias = lax.fori_loop(0, cap, add, jnp.zeros((wall, gstep), F32), unroll=True)
        for k in range(gstep // width):
            d = c * (gstep // width) + k
            part[d] = bias[:, k * width : (k + 1) * width]
            copy = send(part.at[d], part_got.at[me], r_send.at[d], r_recv.at[me], d)
            r_copies.append(copy)
            pl.when(me != d)(copy.start)
    part_got[me] = part[me]
    for off in range(1, n):
        src = lax.rem(me + n - off, n)
        send(part.at[src], part_got.at[src], r_send.at[src], r_recv.at[src], src).wait_recv()
    bias = part_got[0]
    for s in range(1, n):
        bias = bias + part_got[s]
    drawn = jnp.zeros((wall, width), jnp.int32)
    group = jnp.zeros((1, width), jnp.int32)
    for d in range(n):
        drawn = jnp.where(me == d, aux_ref[:, d * width : (d + 1) * width], drawn)
        group = jnp.where(me == d, cgroup_ref[:, d * width : (d + 1) * width], group)
    weight = jnp.zeros((1, width), F32)
    for k in range(gweight_ref.shape[0]):
        weight = jnp.where(group == k, gweight_ref[k], weight)
    sampled = drawn.astype(F32) * (1.0 / 262144.0)
    field_own[...] = (weight * (sampled - bias)).astype(BF)
    f_copies, l_copies = [], []
    for off in range(1, n):
        dst = lax.rem(me + off, n)
        f_copies.append(send(field_own, field_got.at[me], f_send.at[off], f_recv.at[off], dst))
        f_copies[-1].start()
    logw = jnp.sum(sampled * bias - 0.5 * bias * bias, axis=1, keepdims=True)
    logw_own[...] = jnp.broadcast_to(logw, logw_own.shape)
    for off in range(1, n):
        dst = lax.rem(me + off, n)
        l_copies.append(send(logw_own, logw_got.at[me], l_send.at[off], l_recv.at[off], dst))
        l_copies[-1].start()
    field_got[me] = field_own[...]
    logw_got[me] = logw_own[...]
    for copy in f_copies:
        copy.wait_recv()
    for s in range(n):
        field_all[:, s * width : (s + 1) * width] = field_got[s]

    def spread(j, carry):
        pot_v[j] = dot(field_all[...], chol_v[j]).astype(BF)
        return carry

    lax.fori_loop(0, cap, spread, 0, unroll=True)
    for j in range(cap, slots):
        pot_v[j] = jnp.zeros((wall, entries), BF)
    back[...] = dot(swap_matrix(wall, slots), pot_v[...].reshape(rows, entries)).astype(
        BF
    ).reshape(n, slots, entries)
    b_copies = []
    for off in range(1, n):
        dst = lax.rem(me + off, n)
        b_copies.append(send(back.at[dst], back_got.at[me], b_send.at[off], b_recv.at[off], dst))
        b_copies[-1].start()
    back_got[me] = back[me]

    for copy in l_copies:
        copy.wait_recv()
    logw = logw_got[0]
    for s in range(1, n):
        logw = logw + logw_got[s]
    mine = (iota(logw.shape, 0) == me) & (iota(logw.shape, 1) == 0)
    lw_ref[0] = jnp.sum(jnp.where(mine, logw, 0.0))
    gather = hot(iota((ntile, rows), 0) == lane_tile)
    unfold = hot(mod(iota((entries, orbitals), 0), side) == mod(iota((entries, orbitals), 1), side))
    unperm = swap_matrix(NBLK, side)

    for copy in b_copies:
        copy.wait_recv()
    pot_t = dot(gather, back_got[...].reshape(rows, entries))

    def put(p, carry):
        chosen = jnp.where(entry_row == p, pot_t, 0.0).astype(BF)
        wide = dot(chosen, unfold).astype(BF) * col_mask
        v_mat[pl.ds(pl.multiple_of(p * NBLK, NBLK), NBLK), :] = dot(row_put, wide).astype(BF)
        return carry

    lax.fori_loop(0, side, put, 0, unroll=True)
    v_mat[...] = dot(unperm, v_mat[...]).astype(BF)
    term = walk_ref[0]
    running = term.astype(F32)
    for degree in range(1, 5):
        term = (dot(v_mat[...], term) / degree).astype(BF)
        running = running + term.astype(F32)
    adv_ref[0] = running.astype(BF)

    for copy in a_copies + f_copies + l_copies + b_copies:
        copy.wait_send()
    for d, copy in enumerate(r_copies):
        pl.when(me != d)(copy.wait_send)


def per_device(
    walkers, green_factor, trial, chol, pattern, owner_counts, chol_group, group_weight, aux
):
    n = owner_counts.shape[0]
    cap, nchol, entries = chol.shape
    wall = aux.shape[0]
    assert walkers.shape[0] == 1 and wall == n
    orbitals = walkers.shape[1]
    slots = -(-cap // 16) * 16
    gstep = min(256, nchol)
    width = nchol // n
    dma = pltpu.SemaphoreType.DMA
    vmem = pl.BlockSpec(memory_space=pltpu.VMEM)
    smem = pl.BlockSpec(memory_space=pltpu.SMEM)
    advanced, log_weight = pl.pallas_call(
        functools.partial(kernel, n, cap, slots, gstep),
        out_shape=(
            jax.ShapeDtypeStruct(walkers.shape, BF),
            jax.ShapeDtypeStruct((1,), F32),
        ),
        in_specs=[vmem, vmem, vmem, pl.BlockSpec(memory_space=pl.ANY), vmem, smem, vmem, smem, vmem],
        out_specs=(vmem, smem),
        scratch_shapes=[
            pltpu.VMEM((cap, nchol, entries), BF),
            pltpu.VMEM((n * slots, n * slots), BF),
            pltpu.VMEM((orbitals, orbitals), BF),
            pltpu.VMEM((n, slots, entries), BF),
            pltpu.VMEM((n, slots, entries), BF),
            pltpu.VMEM((slots, wall, entries), BF),
            pltpu.VMEM((n, wall, width), F32),
            pltpu.VMEM((n, wall, width), F32),
            pltpu.VMEM((wall, width), BF),
            pltpu.VMEM((n, wall, width), BF),
            pltpu.VMEM((wall, nchol), BF),
            pltpu.VMEM((wall, 128), F32),
            pltpu.VMEM((n, wall, 128), F32),
            pltpu.VMEM((slots, wall, entries), BF),
            pltpu.VMEM((n, slots, entries), BF),
            pltpu.VMEM((n, slots, entries), BF),
            pltpu.VMEM((orbitals, orbitals), BF),
            dma((nchol // gstep,)),
        ]
        + [dma((n,))] * 10,
        compiler_params=pltpu.CompilerParams(
            collective_id=0, has_side_effects=True, vmem_limit_bytes=56 * 2**20
        ),
        cost_estimate=pl.CostEstimate(
            flops=4 * wall * cap * nchol * entries, bytes_accessed=2 * chol.size, transcendentals=0
        ),
    )(
        walkers, green_factor, trial, chol, pattern.reshape(1, -1), owner_counts,
        chol_group.reshape(1, -1), group_weight, aux,
    )
    return advanced, log_weight


def solution(mesh):
    return jax.shard_map(
        per_device,
        mesh=mesh,
        in_specs=(
            P(("groups", "tile"), None, None),
            P(("groups", "tile"), None, None),
            P(),
            P("tile", None, None),
            P(),
            P(),
            P(),
            P(),
            P("groups", None),
        ),
        out_specs=(P(("groups", "tile"), None, None), P(("groups", "tile"))),
        check_vma=False,
    )
```

```python
import functools

import jax
import jax.numpy as jnp
from jax import lax
from jax.experimental import pallas as pl
from jax.experimental.pallas import tpu as pltpu
from jax.sharding import PartitionSpec as P

NBLK = 32
BF = jnp.bfloat16
F32 = jnp.float32
NT_DIMS = (((1,), (1,)), ((), ()))


def quot(x, k):
    if k & (k - 1) == 0:
        return lax.shift_right_logical(x, jnp.int32(k.bit_length() - 1))
    return lax.div(x, jnp.int32(k))


def mod(x, k):
    if k & (k - 1) == 0:
        return lax.bitwise_and(x, jnp.int32(k - 1))
    return lax.rem(x, jnp.int32(k))


def iota(shape, dim):
    return lax.broadcasted_iota(jnp.int32, shape, dim)


def hot(cond):
    return jnp.where(cond, 1.0, 0.0).astype(BF)


def dot(a, b):
    return jnp.dot(a, b, preferred_element_type=F32)


def swap_matrix(outer, inner):
    size = outer * inner
    row = iota((size, size), 0)
    col = iota((size, size), 1)
    return hot(col == mod(row, inner) * outer + quot(row, inner))


def kernel(
    n, cap, part_size, halves, chunk, gstep,
    walk_ref, factor_ref, trial_ref, chol_ref, pattern_ref, counts_ref, cgroup_ref, gweight_ref,
    aux_ref,
    adv_ref, lw_ref,
    chol_v, spots, green_v, sent, got, tiles_v, bias_acc, part, part_got, field_own, field_got,
    field_all, logw_own, logw_got, pot_acc, pot_v, back, back_got, v_mat,
    chol_sem, a_send, a_recv, r_send, r_recv, f_send, f_recv, l_send, l_recv, b_send, b_recv,
):
    me = lax.axis_index("tile")
    orbitals = walk_ref.shape[1]
    nchol, entries = chol_ref.shape[1], chol_ref.shape[2]
    ntile = pattern_ref.shape[1]
    wall = aux_ref.shape[0]
    side = orbitals // NBLK
    group = chunk // side
    ngroup = NBLK // group
    half = nchol // halves
    nch = half // chunk
    wrows = wall * nch // n
    parts = -(-cap // part_size)
    rows = n * part_size
    mine_k = lax.rem(me, nch)
    others = [lax.rem(me + off, n) for off in range(1, n)]

    def send(src, dst, ssem, rsem, dev):
        return pltpu.make_async_remote_copy(
            src_ref=src, dst_ref=dst, send_sem=ssem, recv_sem=rsem,
            device_id={"tile": dev}, device_id_type=pl.DeviceIdType.MESH,
        )

    barrier = pltpu.get_barrier_semaphore()
    for dst in others:
        pl.semaphore_signal(
            barrier, inc=1, device_id={"tile": dst}, device_id_type=pl.DeviceIdType.MESH
        )
    span = [(jp * part_size, min(cap, (jp + 1) * part_size)) for jp in range(parts)]
    chol_copies = {}
    for jp, (j0, j1) in enumerate(span):
        for h in range(halves):
            piece = (pl.ds(j0, j1 - j0), pl.ds(h * half, half), slice(None))
            chol_copies[jp, h] = pltpu.make_async_copy(
                chol_ref.at[piece], chol_v.at[piece], chol_sem.at[jp, h]
            )
            chol_copies[jp, h].start()

    perm = swap_matrix(side, NBLK)
    factor = dot(perm, factor_ref[0]).astype(BF)
    green = lax.dot_general(
        factor, trial_ref[...], NT_DIMS, preferred_element_type=F32
    ).astype(BF)
    for p in range(side):
        for c in range(ngroup):
            green_v[c * NBLK : (c + 1) * NBLK, p * chunk : (p + 1) * chunk] = green[
                p * NBLK : (p + 1) * NBLK, c * chunk : (c + 1) * chunk
            ]
    pat_row = pattern_ref[...]
    pat_col = jnp.transpose(jnp.broadcast_to(pat_row, (128, ntile)))[:, :1]

    def place(pat):
        return quot(mod(pat, NBLK), group) * NBLK + quot(pat, NBLK)

    pick = hot(place(pat_col) == iota((ntile, ngroup * NBLK), 1))
    put = hot(place(pat_row) == iota((ngroup * NBLK, ntile), 0))
    col_mask = hot(mod(pat_col, group) == quot(iota((ntile, chunk), 1), side))
    col_mask = jnp.concatenate([col_mask] * side, axis=1)
    wide_lane = iota((entries, side * chunk), 1)
    spots[...] = hot(
        iota((entries, side * chunk), 0) == quot(wide_lane, chunk) * side + mod(wide_lane, side)
    )
    chosen = dot(pick, green_v[...]).astype(BF) * col_mask
    green_t = lax.dot_general(chosen, spots[...], NT_DIMS, preferred_element_type=F32).astype(BF)

    first = jnp.int32(0)
    lane = iota((1, rows), 1)
    slot = iota((part_size, ntile), 0)
    tile_lane = iota((part_size, ntile), 1)
    lane_tile = [jnp.full((1, rows), -1, jnp.int32) for _ in range(parts)]
    own = [[] for _ in range(parts)]
    for d in range(n):
        held = counts_ref[d]
        for jp in range(parts):
            at = slot + jp * part_size
            own[jp].append(jnp.where((tile_lane == at + first) & (at < held), 1.0, 0.0))
            in_part = lane - d * part_size
            at = in_part + jp * part_size
            live = (in_part >= 0) & (in_part < part_size) & (at < held)
            lane_tile[jp] = jnp.where(live, at + first, lane_tile[jp])
        first = first + held

    a_copies = [[] for _ in range(parts)]
    for jp in range(parts):
        rows_out = dot(jnp.concatenate(own[jp], axis=0).astype(BF), green_t)
        sent[jp] = rows_out.astype(BF).reshape(n, part_size, entries)
        if jp == 0:
            pl.semaphore_wait(barrier, n - 1)
        for i, dst in enumerate(others):
            copy = send(
                sent.at[jp, dst], got.at[jp, me], a_send.at[jp, i], a_recv.at[jp, i], dst
            )
            copy.start()
            a_copies[jp].append(copy)
        got[jp, me] = sent[jp, me]

    r_copies, f_copies, l_copies = [], [[] for _ in range(halves)], []
    logw_parts = []

    def bias_block(jp, h, g):
        j0, j1 = span[jp]
        g0 = h * half + g * gstep
        total = bias_acc[:, g0 : g0 + gstep] if jp else jnp.zeros((wall, gstep), F32)
        for j in range(j0, j1):
            total = total + lax.dot_general(
                tiles_v[j], chol_v[j, g0 : g0 + gstep, :], NT_DIMS, preferred_element_type=F32
            )
        if jp < parts - 1:
            bias_acc[:, g0 : g0 + gstep] = total
            return
        for k in range(gstep // chunk):
            kk = g * (gstep // chunk) + k
            part[h, kk] = total[:, k * chunk : (k + 1) * chunk]
            for wg in range(n // nch):
                d = wg * nch + kk
                copy = send(
                    part.at[h, kk, wg * wrows : (wg + 1) * wrows], part_got.at[h, me],
                    r_send.at[h, d], r_recv.at[h, me], d,
                )
                r_copies.append((d, copy))
                pl.when(me != d)(copy.start)

                @pl.when(me == d)
                def _():
                    part_got[h, me] = part[h, kk, wg * wrows : (wg + 1) * wrows]

    def reduce_bias(h):
        for src in others:
            send(
                part.at[h, 0, 0:wrows], part_got.at[h, src], r_send.at[h, src],
                r_recv.at[h, src], src,
            ).wait_recv()
        bias = part_got[h, 0]
        for s in range(1, n):
            bias = bias + part_got[h, s]
        drawn = jnp.zeros((wrows, chunk), jnp.int32)
        kind = jnp.zeros((1, chunk), jnp.int32)
        for d in range(n):
            g0 = h * half + (d % nch) * chunk
            w0 = (d // nch) * wrows
            drawn = jnp.where(me == d, aux_ref[w0 : w0 + wrows, g0 : g0 + chunk], drawn)
            kind = jnp.where(me == d, cgroup_ref[:, g0 : g0 + chunk], kind)
        weight = jnp.zeros((1, chunk), F32)
        for k in range(gweight_ref.shape[0]):
            weight = jnp.where(kind == k, gweight_ref[k], weight)
        sampled = drawn.astype(F32) * (1.0 / 262144.0)
        field_own[h] = (weight * (sampled - bias)).astype(BF).astype(F32)
        for i, dst in enumerate(others):
            copy = send(
                field_own.at[h], field_got.at[h, me], f_send.at[h, i], f_recv.at[h, i], dst
            )
            copy.start()
            f_copies[h].append(copy)
        field_got[h, me] = field_own[h]
        logw_parts.append(
            jnp.sum(sampled * bias - 0.5 * bias * bias, axis=1, keepdims=True)
        )

    def gather_fields(h):
        for copy in f_copies[h]:
            copy.wait_recv()
        for s in range(n):
            g0 = h * half + (s % nch) * chunk
            w0 = (s // nch) * wrows
            field_all[w0 : w0 + wrows, g0 : g0 + chunk] = field_got[h, s]
        return field_all[:, h * half : (h + 1) * half].astype(BF)

    blocks = half // gstep
    for jp in range(parts):
        for copy in a_copies[jp]:
            copy.wait_recv()
        j0 = jp * part_size
        tiles_v[j0 : j0 + part_size] = dot(
            swap_matrix(part_size, wall), got[jp].reshape(rows, entries)
        ).astype(BF).reshape(part_size, wall, entries)
        for h in range(halves):
            chol_copies[jp, h].wait()
            for g in range(blocks):
                if jp == parts - 1 and h > 0 and g == blocks - 1:
                    reduce_bias(h - 1)
                bias_block(jp, h, g)

    fields = gather_fields(0)
    for h in range(halves - 1):
        for jp, (j0, j1) in enumerate(span):
            for j in range(j0, j1):
                new = dot(fields, chol_v[j, h * half : (h + 1) * half, :])
                pot_acc[j] = new if h == 0 else pot_acc[j] + new
            if jp == 0 and h == halves - 2:
                reduce_bias(halves - 1)
        fields = gather_fields(h + 1)
    b_copies = [[] for _ in range(parts)]
    h = halves - 1
    for jp, (j0, j1) in enumerate(span):
        for j in range(j0, j1):
            pot_v[j] = (
                pot_acc[j] + dot(fields, chol_v[j, h * half : (h + 1) * half, :])
            ).astype(BF)
        for j in range(j1, j0 + part_size):
            pot_v[j] = jnp.zeros((wall, entries), BF)
        back[jp] = dot(
            swap_matrix(wall, part_size), pot_v[j0 : j0 + part_size].reshape(rows, entries)
        ).astype(BF).reshape(n, part_size, entries)
        for i, dst in enumerate(others):
            copy = send(
                back.at[jp, dst], back_got.at[jp, me], b_send.at[jp, i], b_recv.at[jp, i], dst
            )
            copy.start()
            b_copies[jp].append(copy)
        back_got[jp, me] = back[jp, me]

    logw = sum(logw_parts[1:], logw_parts[0])
    logw_own[...] = jnp.broadcast_to(logw, logw_own.shape)
    for off in range(1, nch):
        dst = me - mine_k + lax.rem(mine_k + off, nch)
        copy = send(logw_own, logw_got.at[mine_k], l_send.at[off], l_recv.at[off], dst)
        copy.start()
        l_copies.append(copy)
    logw_got[mine_k] = logw_own[...]
    unperm = swap_matrix(NBLK, side)
    gather = [hot(iota((ntile, rows), 0) == lane_tile[jp]) for jp in range(parts)]

    pot_t = jnp.zeros((ntile, entries), F32)
    for jp in range(parts):
        for copy in b_copies[jp]:
            copy.wait_recv()
        pot_t = pot_t + dot(gather[jp], back_got[jp].reshape(rows, entries))
    wide = dot(pot_t.astype(BF), spots[...]).astype(BF) * col_mask
    placed = dot(put, wide).astype(BF)
    for p in range(side):
        for c in range(ngroup):
            v_mat[p * NBLK : (p + 1) * NBLK, c * chunk : (c + 1) * chunk] = placed[
                c * NBLK : (c + 1) * NBLK, p * chunk : (p + 1) * chunk
            ]
    v_mat[...] = dot(unperm, v_mat[...]).astype(BF)
    term = walk_ref[0]
    running = term.astype(F32)
    for degree in range(1, 5):
        term = (dot(v_mat[...], term) / degree).astype(BF)
        running = running + term.astype(F32)
    adv_ref[0] = running.astype(BF)

    for copy in l_copies:
        copy.wait_recv()
    logw = logw_got[0]
    for s in range(1, nch):
        logw = logw + logw_got[s]
    mine = (iota(logw.shape, 0) == lax.rem(me, wrows)) & (iota(logw.shape, 1) == 0)
    lw_ref[0] = jnp.sum(jnp.where(mine, logw, 0.0))
    for copy in sum(a_copies + f_copies + b_copies, l_copies):
        copy.wait_send()
    for d, copy in r_copies:
        pl.when(me != d)(copy.wait_send)


def per_device(
    walkers, green_factor, trial, chol, pattern, owner_counts, chol_group, group_weight, aux
):
    n = owner_counts.shape[0]
    cap, nchol, entries = chol.shape
    wall = aux.shape[0]
    assert walkers.shape[0] == 1 and wall == n
    orbitals = walkers.shape[1]
    chunk, part_size, halves, gstep = 128, 16, 2, 256
    nch = nchol // halves // chunk
    assert n % nch == 0
    parts = -(-cap // part_size)
    side = orbitals // NBLK
    wrows = wall * nch // n
    dma = pltpu.SemaphoreType.DMA
    vmem = pl.BlockSpec(memory_space=pltpu.VMEM)
    smem = pl.BlockSpec(memory_space=pltpu.SMEM)
    advanced, log_weight = pl.pallas_call(
        functools.partial(kernel, n, cap, part_size, halves, chunk, gstep),
        out_shape=(
            jax.ShapeDtypeStruct(walkers.shape, BF),
            jax.ShapeDtypeStruct((1,), F32),
        ),
        in_specs=[vmem, vmem, vmem, pl.BlockSpec(memory_space=pl.ANY), vmem, smem, vmem, smem, vmem],
        out_specs=(vmem, smem),
        scratch_shapes=[
            pltpu.VMEM((cap, nchol, entries), BF),
            pltpu.VMEM((entries, side * chunk), BF),
            pltpu.VMEM((orbitals // chunk * NBLK, side * chunk), BF),
            pltpu.VMEM((parts, n, part_size, entries), BF),
            pltpu.VMEM((parts, n, part_size, entries), BF),
            pltpu.VMEM((parts * part_size, wall, entries), BF),
            pltpu.VMEM((wall, nchol), F32),
            pltpu.VMEM((halves, nch, wall, chunk), F32),
            pltpu.VMEM((halves, n, wrows, chunk), F32),
            pltpu.VMEM((halves, wrows, chunk), F32),
            pltpu.VMEM((halves, n, wrows, chunk), F32),
            pltpu.VMEM((wall, nchol), F32),
            pltpu.VMEM((wrows, chunk), F32),
            pltpu.VMEM((nch, wrows, chunk), F32),
            pltpu.VMEM((cap, wall, entries), F32),
            pltpu.VMEM((parts * part_size, wall, entries), BF),
            pltpu.VMEM((parts, n, part_size, entries), BF),
            pltpu.VMEM((parts, n, part_size, entries), BF),
            pltpu.VMEM((orbitals, orbitals), BF),
            dma((parts, halves)),
            dma((parts, n)), dma((parts, n)),
            dma((halves, n)), dma((halves, n)),
            dma((halves, n)), dma((halves, n)),
            dma((nch,)), dma((nch,)),
            dma((parts, n)), dma((parts, n)),
        ],
        compiler_params=pltpu.CompilerParams(
            collective_id=0, has_side_effects=True, vmem_limit_bytes=56 * 2**20
        ),
        cost_estimate=pl.CostEstimate(
            flops=4 * wall * cap * nchol * entries, bytes_accessed=2 * chol.size, transcendentals=0
        ),
    )(
        walkers, green_factor, trial, chol, pattern.reshape(1, -1), owner_counts,
        chol_group.reshape(1, -1), group_weight, aux,
    )
    return advanced, log_weight


def solution(mesh):
    return jax.shard_map(
        per_device,
        mesh=mesh,
        in_specs=(
            P(("groups", "tile"), None, None),
            P(("groups", "tile"), None, None),
            P(),
            P("tile", None, None),
            P(),
            P(),
            P(),
            P(),
            P("groups", None),
        ),
        out_specs=(P(("groups", "tile"), None, None), P(("groups", "tile"))),
        check_vma=False,
    )
```

```python
import functools

import jax
import jax.numpy as jnp
from jax import lax
from jax.experimental import pallas as pl
from jax.experimental.pallas import tpu as pltpu
from jax.sharding import PartitionSpec as P

NBLK = 32
BF = jnp.bfloat16
F32 = jnp.float32
NT_DIMS = (((1,), (1,)), ((), ()))


def quot(x, k):
    if k & (k - 1) == 0:
        return lax.shift_right_logical(x, jnp.int32(k.bit_length() - 1))
    return lax.div(x, jnp.int32(k))


def mod(x, k):
    if k & (k - 1) == 0:
        return lax.bitwise_and(x, jnp.int32(k - 1))
    return lax.rem(x, jnp.int32(k))


def iota(shape, dim):
    return lax.broadcasted_iota(jnp.int32, shape, dim)


def hot(cond):
    return jnp.where(cond, 1.0, 0.0).astype(BF)


def dot(a, b):
    return jnp.dot(a, b, preferred_element_type=F32)


def swap_matrix(outer, inner):
    size = outer * inner
    row = iota((size, size), 0)
    col = iota((size, size), 1)
    return hot(col == mod(row, inner) * outer + quot(row, inner))


def kernel(
    n, cap, part_size, halves, chunk,
    walk_ref, factor_ref, trial_ref, chol_ref, pattern_ref, counts_ref, cgroup_ref, gweight_ref,
    aux_ref,
    adv_ref, lw_ref,
    chol_v, spots, green_v, sent, got, tiles_v, bias_acc, part, part_got, field_own, field_got,
    field_all, logw_own, logw_got, pot_acc, pot_v, back, back_got, v_mat,
    chol_sem, a_send, a_recv, r_send, r_recv, f_send, f_recv, l_send, l_recv, b_send, b_recv,
):
    me = lax.axis_index("tile")
    orbitals = walk_ref.shape[1]
    nchol, entries = chol_ref.shape[1], chol_ref.shape[2]
    ntile = pattern_ref.shape[1]
    wall = aux_ref.shape[0]
    side = orbitals // NBLK
    group = chunk // side
    ngroup = NBLK // group
    half = nchol // halves
    nch = half // chunk
    wrows = wall * nch // n
    parts = -(-cap // part_size)
    rows = n * part_size
    mine_k = lax.rem(me, nch)
    others = [lax.rem(me + off, n) for off in range(1, n)]

    def send(src, dst, ssem, rsem, dev):
        return pltpu.make_async_remote_copy(
            src_ref=src, dst_ref=dst, send_sem=ssem, recv_sem=rsem,
            device_id={"tile": dev}, device_id_type=pl.DeviceIdType.MESH,
        )

    barrier = pltpu.get_barrier_semaphore()
    for dst in others:
        pl.semaphore_signal(
            barrier, inc=1, device_id={"tile": dst}, device_id_type=pl.DeviceIdType.MESH
        )
    span = [(jp * part_size, min(cap, (jp + 1) * part_size)) for jp in range(parts)]
    chol_copies = {}
    for jp, (j0, j1) in enumerate(span):
        for h in range(halves):
            piece = (pl.ds(j0, j1 - j0), pl.ds(h * half, half), slice(None))
            chol_copies[jp, h] = pltpu.make_async_copy(
                chol_ref.at[piece], chol_v.at[piece], chol_sem.at[jp, h]
            )
            chol_copies[jp, h].start()

    perm = swap_matrix(side, NBLK)
    factor = dot(perm, factor_ref[0]).astype(BF)
    green = lax.dot_general(
        factor, trial_ref[...], NT_DIMS, preferred_element_type=F32
    ).astype(BF)
    for p in range(side):
        for c in range(ngroup):
            green_v[c * NBLK : (c + 1) * NBLK, p * chunk : (p + 1) * chunk] = green[
                p * NBLK : (p + 1) * NBLK, c * chunk : (c + 1) * chunk
            ]
    pat_row = pattern_ref[...]
    pat_col = jnp.transpose(jnp.broadcast_to(pat_row, (128, ntile)))[:, :1]

    def place(pat):
        return quot(mod(pat, NBLK), group) * NBLK + quot(pat, NBLK)

    pick = hot(place(pat_col) == iota((ntile, ngroup * NBLK), 1))
    put = hot(place(pat_row) == iota((ngroup * NBLK, ntile), 0))
    col_mask = hot(mod(pat_col, group) == quot(iota((ntile, chunk), 1), side))
    col_mask = jnp.concatenate([col_mask] * side, axis=1)
    wide_lane = iota((entries, side * chunk), 1)
    spots[...] = hot(
        iota((entries, side * chunk), 0) == quot(wide_lane, chunk) * side + mod(wide_lane, side)
    )
    chosen = dot(pick, green_v[...]).astype(BF) * col_mask
    green_t = lax.dot_general(chosen, spots[...], NT_DIMS, preferred_element_type=F32).astype(BF)

    first = jnp.int32(0)
    lane = iota((1, rows), 1)
    slot = iota((part_size, ntile), 0)
    tile_lane = iota((part_size, ntile), 1)
    lane_tile = [jnp.full((1, rows), -1, jnp.int32) for _ in range(parts)]
    own = [[] for _ in range(parts)]
    for d in range(n):
        held = counts_ref[d]
        for jp in range(parts):
            at = slot + jp * part_size
            own[jp].append(jnp.where((tile_lane == at + first) & (at < held), 1.0, 0.0))
            in_part = lane - d * part_size
            at = in_part + jp * part_size
            live = (in_part >= 0) & (in_part < part_size) & (at < held)
            lane_tile[jp] = jnp.where(live, at + first, lane_tile[jp])
        first = first + held

    a_copies = [[] for _ in range(parts)]
    for jp in range(parts):
        rows_out = dot(jnp.concatenate(own[jp], axis=0).astype(BF), green_t)
        sent[jp] = rows_out.astype(BF).reshape(n, part_size, entries)
        if jp == 0:
            pl.semaphore_wait(barrier, n - 1)
        for i, dst in enumerate(others):
            copy = send(
                sent.at[jp, dst], got.at[jp, me], a_send.at[jp, i], a_recv.at[jp, i], dst
            )
            copy.start()
            a_copies[jp].append(copy)
        got[jp, me] = sent[jp, me]

    r_copies, f_copies, l_copies = [], [[] for _ in range(halves)], []
    logw_parts = []

    def bias_half(jp, h):
        j0, j1 = span[jp]
        g0 = h * half
        for j in range(j0, j1):
            new = lax.dot_general(
                chol_v[j, g0 : g0 + half, :], tiles_v[j], NT_DIMS, preferred_element_type=F32
            )
            bias_acc[g0 : g0 + half, :] = bias_acc[g0 : g0 + half, :] + new if j else new
        if jp < parts - 1:
            return
        for kk in range(nch):
            part[h, kk] = jnp.transpose(
                bias_acc[g0 + kk * chunk : g0 + (kk + 1) * chunk, :]
            )
            for wg in range(n // nch):
                d = wg * nch + kk
                copy = send(
                    part.at[h, kk, wg * wrows : (wg + 1) * wrows], part_got.at[h, me],
                    r_send.at[h, d], r_recv.at[h, me], d,
                )
                r_copies.append((d, copy))
                pl.when(me != d)(copy.start)

                @pl.when(me == d)
                def _():
                    part_got[h, me] = part[h, kk, wg * wrows : (wg + 1) * wrows]

    def reduce_bias(h):
        for src in others:
            send(
                part.at[h, 0, 0:wrows], part_got.at[h, src], r_send.at[h, src],
                r_recv.at[h, src], src,
            ).wait_recv()
        bias = part_got[h, 0]
        for s in range(1, n):
            bias = bias + part_got[h, s]
        drawn = jnp.zeros((wrows, chunk), jnp.int32)
        kind = jnp.zeros((1, chunk), jnp.int32)
        for d in range(n):
            g0 = h * half + (d % nch) * chunk
            w0 = (d // nch) * wrows
            drawn = jnp.where(me == d, aux_ref[w0 : w0 + wrows, g0 : g0 + chunk], drawn)
            kind = jnp.where(me == d, cgroup_ref[:, g0 : g0 + chunk], kind)
        weight = jnp.zeros((1, chunk), F32)
        for k in range(gweight_ref.shape[0]):
            weight = jnp.where(kind == k, gweight_ref[k], weight)
        sampled = drawn.astype(F32) * (1.0 / 262144.0)
        field_own[h] = (weight * (sampled - bias)).astype(BF).astype(F32)
        for i, dst in enumerate(others):
            copy = send(
                field_own.at[h], field_got.at[h, me], f_send.at[h, i], f_recv.at[h, i], dst
            )
            copy.start()
            f_copies[h].append(copy)
        field_got[h, me] = field_own[h]
        logw_parts.append(
            jnp.sum(sampled * bias - 0.5 * bias * bias, axis=1, keepdims=True)
        )

    def gather_fields(h):
        for copy in f_copies[h]:
            copy.wait_recv()
        for s in range(n):
            g0 = h * half + (s % nch) * chunk
            w0 = (s // nch) * wrows
            field_all[w0 : w0 + wrows, g0 : g0 + chunk] = field_got[h, s]
        return field_all[:, h * half : (h + 1) * half].astype(BF)

    for jp in range(parts):
        for copy in a_copies[jp]:
            copy.wait_recv()
        j0 = jp * part_size
        tiles_v[j0 : j0 + part_size] = dot(
            swap_matrix(part_size, wall), got[jp].reshape(rows, entries)
        ).astype(BF).reshape(part_size, wall, entries)
        for h in range(halves):
            chol_copies[jp, h].wait()
            bias_half(jp, h)
            if jp == parts - 1 and h > 0:
                reduce_bias(h - 1)

    fields = gather_fields(0)
    for h in range(halves - 1):
        for jp, (j0, j1) in enumerate(span):
            for j in range(j0, j1):
                new = dot(fields, chol_v[j, h * half : (h + 1) * half, :])
                pot_acc[j] = new if h == 0 else pot_acc[j] + new
            if jp == 0 and h == halves - 2:
                reduce_bias(halves - 1)
        fields = gather_fields(h + 1)
    b_copies = [[] for _ in range(parts)]
    h = halves - 1
    for jp, (j0, j1) in enumerate(span):
        for j in range(j0, j1):
            pot_v[j] = (
                pot_acc[j] + dot(fields, chol_v[j, h * half : (h + 1) * half, :])
            ).astype(BF)
        for j in range(j1, j0 + part_size):
            pot_v[j] = jnp.zeros((wall, entries), BF)
        back[jp] = dot(
            swap_matrix(wall, part_size), pot_v[j0 : j0 + part_size].reshape(rows, entries)
        ).astype(BF).reshape(n, part_size, entries)
        for i, dst in enumerate(others):
            copy = send(
                back.at[jp, dst], back_got.at[jp, me], b_send.at[jp, i], b_recv.at[jp, i], dst
            )
            copy.start()
            b_copies[jp].append(copy)
        back_got[jp, me] = back[jp, me]

    logw = sum(logw_parts[1:], logw_parts[0])
    logw_own[...] = jnp.broadcast_to(logw, logw_own.shape)
    for off in range(1, nch):
        dst = me - mine_k + lax.rem(mine_k + off, nch)
        copy = send(logw_own, logw_got.at[mine_k], l_send.at[off], l_recv.at[off], dst)
        copy.start()
        l_copies.append(copy)
    logw_got[mine_k] = logw_own[...]
    unperm = swap_matrix(NBLK, side)
    gather = [hot(iota((ntile, rows), 0) == lane_tile[jp]) for jp in range(parts)]

    pot_t = jnp.zeros((ntile, entries), F32)
    for jp in range(parts):
        for copy in b_copies[jp]:
            copy.wait_recv()
        pot_t = pot_t + dot(gather[jp], back_got[jp].reshape(rows, entries))
    wide = dot(pot_t.astype(BF), spots[...]).astype(BF) * col_mask
    placed = dot(put, wide).astype(BF)
    for p in range(side):
        for c in range(ngroup):
            v_mat[p * NBLK : (p + 1) * NBLK, c * chunk : (c + 1) * chunk] = placed[
                c * NBLK : (c + 1) * NBLK, p * chunk : (p + 1) * chunk
            ]
    v_mat[...] = dot(unperm, v_mat[...]).astype(BF)
    term = walk_ref[0]
    running = term.astype(F32)
    for degree in range(1, 5):
        term = (dot(v_mat[...], term) / degree).astype(BF)
        running = running + term.astype(F32)
    adv_ref[0] = running.astype(BF)

    for copy in l_copies:
        copy.wait_recv()
    logw = logw_got[0]
    for s in range(1, nch):
        logw = logw + logw_got[s]
    mine = (iota(logw.shape, 0) == lax.rem(me, wrows)) & (iota(logw.shape, 1) == 0)
    lw_ref[0] = jnp.sum(jnp.where(mine, logw, 0.0))
    for copy in sum(a_copies + f_copies + b_copies, l_copies):
        copy.wait_send()
    for d, copy in r_copies:
        pl.when(me != d)(copy.wait_send)


def per_device(
    walkers, green_factor, trial, chol, pattern, owner_counts, chol_group, group_weight, aux
):
    n = owner_counts.shape[0]
    cap, nchol, entries = chol.shape
    wall = aux.shape[0]
    assert walkers.shape[0] == 1 and wall == n
    orbitals = walkers.shape[1]
    chunk, part_size, halves = 128, 16, 2
    nch = nchol // halves // chunk
    assert n % nch == 0
    parts = -(-cap // part_size)
    side = orbitals // NBLK
    wrows = wall * nch // n
    dma = pltpu.SemaphoreType.DMA
    vmem = pl.BlockSpec(memory_space=pltpu.VMEM)
    smem = pl.BlockSpec(memory_space=pltpu.SMEM)
    advanced, log_weight = pl.pallas_call(
        functools.partial(kernel, n, cap, part_size, halves, chunk),
        out_shape=(
            jax.ShapeDtypeStruct(walkers.shape, BF),
            jax.ShapeDtypeStruct((1,), F32),
        ),
        in_specs=[vmem, vmem, vmem, pl.BlockSpec(memory_space=pl.ANY), vmem, smem, vmem, smem, vmem],
        out_specs=(vmem, smem),
        scratch_shapes=[
            pltpu.VMEM((cap, nchol, entries), BF),
            pltpu.VMEM((entries, side * chunk), BF),
            pltpu.VMEM((orbitals // chunk * NBLK, side * chunk), BF),
            pltpu.VMEM((parts, n, part_size, entries), BF),
            pltpu.VMEM((parts, n, part_size, entries), BF),
            pltpu.VMEM((parts * part_size, wall, entries), BF),
            pltpu.VMEM((nchol, wall), F32),
            pltpu.VMEM((halves, nch, wall, chunk), F32),
            pltpu.VMEM((halves, n, wrows, chunk), F32),
            pltpu.VMEM((halves, wrows, chunk), F32),
            pltpu.VMEM((halves, n, wrows, chunk), F32),
            pltpu.VMEM((wall, nchol), F32),
            pltpu.VMEM((wrows, chunk), F32),
            pltpu.VMEM((nch, wrows, chunk), F32),
            pltpu.VMEM((cap, wall, entries), F32),
            pltpu.VMEM((parts * part_size, wall, entries), BF),
            pltpu.VMEM((parts, n, part_size, entries), BF),
            pltpu.VMEM((parts, n, part_size, entries), BF),
            pltpu.VMEM((orbitals, orbitals), BF),
            dma((parts, halves)),
            dma((parts, n)), dma((parts, n)),
            dma((halves, n)), dma((halves, n)),
            dma((halves, n)), dma((halves, n)),
            dma((nch,)), dma((nch,)),
            dma((parts, n)), dma((parts, n)),
        ],
        compiler_params=pltpu.CompilerParams(
            collective_id=0, has_side_effects=True, vmem_limit_bytes=56 * 2**20
        ),
        cost_estimate=pl.CostEstimate(
            flops=4 * wall * cap * nchol * entries, bytes_accessed=2 * chol.size, transcendentals=0
        ),
    )(
        walkers, green_factor, trial, chol, pattern.reshape(1, -1), owner_counts,
        chol_group.reshape(1, -1), group_weight, aux,
    )
    return advanced, log_weight


def solution(mesh):
    return jax.shard_map(
        per_device,
        mesh=mesh,
        in_specs=(
            P(("groups", "tile"), None, None),
            P(("groups", "tile"), None, None),
            P(),
            P("tile", None, None),
            P(),
            P(),
            P(),
            P(),
            P("groups", None),
        ),
        out_specs=(P(("groups", "tile"), None, None), P(("groups", "tile"))),
        check_vma=False,
    )
```

```python
import functools

import jax
import jax.numpy as jnp
from jax import lax
from jax.experimental import pallas as pl
from jax.experimental.pallas import tpu as pltpu
from jax.sharding import PartitionSpec as P

NBLK = 32
BF = jnp.bfloat16
F32 = jnp.float32
NT_DIMS = (((1,), (1,)), ((), ()))


def quot(x, k):
    if k & (k - 1) == 0:
        return lax.shift_right_logical(x, jnp.int32(k.bit_length() - 1))
    return lax.div(x, jnp.int32(k))


def mod(x, k):
    if k & (k - 1) == 0:
        return lax.bitwise_and(x, jnp.int32(k - 1))
    return lax.rem(x, jnp.int32(k))


def iota(shape, dim):
    return lax.broadcasted_iota(jnp.int32, shape, dim)


def hot(cond):
    return jnp.where(cond, 1.0, 0.0).astype(BF)


def dot(a, b):
    return jnp.dot(a, b, preferred_element_type=F32)


def swap_matrix(outer, inner):
    size = outer * inner
    row = iota((size, size), 0)
    col = iota((size, size), 1)
    return hot(col == mod(row, inner) * outer + quot(row, inner))


def kernel(
    n, cap, part_size, halves, chunk,
    walk_ref, factor_ref, trial_ref, chol_ref, pattern_ref, counts_ref, cgroup_ref, gweight_ref,
    aux_ref,
    adv_ref, lw_ref,
    chol_v, spots, green_v, sent, got, tiles_v, bias_acc, part, part_got, field_own, field_got,
    field_all, fields_v, logw_own, logw_got, pot_acc, pot_v, back, back_got, v_mat, term_v, running_v,
    chol_sem, a_send, a_recv, r_send, r_recv, f_send, f_recv, l_send, l_recv, b_send, b_recv,
):
    me = lax.axis_index("tile")
    orbitals = walk_ref.shape[1]
    nchol, entries = chol_ref.shape[1], chol_ref.shape[2]
    ntile = pattern_ref.shape[1]
    wall = aux_ref.shape[0]
    side = orbitals // NBLK
    group = chunk // side
    ngroup = NBLK // group
    half = nchol // halves
    nch = half // chunk
    wrows = wall * nch // n
    parts = -(-cap // part_size)
    rows = n * part_size
    mine_k = lax.rem(me, nch)
    others = [lax.rem(me + off, n) for off in range(1, n)]

    def send(src, dst, ssem, rsem, dev):
        return pltpu.make_async_remote_copy(
            src_ref=src, dst_ref=dst, send_sem=ssem, recv_sem=rsem,
            device_id={"tile": dev}, device_id_type=pl.DeviceIdType.MESH,
        )

    barrier = pltpu.get_barrier_semaphore()
    for dst in others:
        pl.semaphore_signal(
            barrier, inc=1, device_id={"tile": dst}, device_id_type=pl.DeviceIdType.MESH
        )
    span = [(jp * part_size, min(cap, (jp + 1) * part_size)) for jp in range(parts)]
    chol_copies = {}
    for jp, (j0, j1) in enumerate(span):
        for h in range(halves):
            piece = (pl.ds(j0, j1 - j0), pl.ds(h * half, half), slice(None))
            chol_copies[jp, h] = pltpu.make_async_copy(
                chol_ref.at[piece], chol_v.at[piece], chol_sem.at[jp, h]
            )
            chol_copies[jp, h].start()

    perm = swap_matrix(side, NBLK)
    factor = dot(perm, factor_ref[0]).astype(BF)
    green = lax.dot_general(
        factor, trial_ref[...], NT_DIMS, preferred_element_type=F32
    ).astype(BF)
    for p in range(side):
        for c in range(ngroup):
            green_v[c * NBLK : (c + 1) * NBLK, p * chunk : (p + 1) * chunk] = green[
                p * NBLK : (p + 1) * NBLK, c * chunk : (c + 1) * chunk
            ]
    pat_row = pattern_ref[...]
    pat_col = jnp.transpose(jnp.broadcast_to(pat_row, (128, ntile)))[:, :1]

    def place(pat):
        return quot(mod(pat, NBLK), group) * NBLK + quot(pat, NBLK)

    pick = hot(place(pat_col) == iota((ntile, ngroup * NBLK), 1))
    put = hot(place(pat_row) == iota((ngroup * NBLK, ntile), 0))
    col_mask = hot(mod(pat_col, group) == quot(iota((ntile, chunk), 1), side))
    col_mask = jnp.concatenate([col_mask] * side, axis=1)
    wide_lane = iota((entries, side * chunk), 1)
    spots[...] = hot(
        iota((entries, side * chunk), 0) == quot(wide_lane, chunk) * side + mod(wide_lane, side)
    )
    chosen = dot(pick, green_v[...]).astype(BF) * col_mask
    green_t = lax.dot_general(chosen, spots[...], NT_DIMS, preferred_element_type=F32).astype(BF)

    first = jnp.int32(0)
    lane = iota((1, rows), 1)
    slot = iota((part_size, ntile), 0)
    tile_lane = iota((part_size, ntile), 1)
    lane_tile = [jnp.full((1, rows), -1, jnp.int32) for _ in range(parts)]
    own = [[] for _ in range(parts)]
    for d in range(n):
        held = counts_ref[d]
        for jp in range(parts):
            at = slot + jp * part_size
            own[jp].append(jnp.where((tile_lane == at + first) & (at < held), 1.0, 0.0))
            in_part = lane - d * part_size
            at = in_part + jp * part_size
            live = (in_part >= 0) & (in_part < part_size) & (at < held)
            lane_tile[jp] = jnp.where(live, at + first, lane_tile[jp])
        first = first + held

    a_copies = [[] for _ in range(parts)]
    for jp in range(parts):
        rows_out = dot(jnp.concatenate(own[jp], axis=0).astype(BF), green_t)
        sent[jp] = rows_out.astype(BF).reshape(n, part_size, entries)
        if jp == 0:
            pl.semaphore_wait(barrier, n - 1)
        for i, dst in enumerate(others):
            copy = send(
                sent.at[jp, dst], got.at[jp, me], a_send.at[jp, i], a_recv.at[jp, i], dst
            )
            copy.start()
            a_copies[jp].append(copy)
        got[jp, me] = sent[jp, me]

    r_copies, f_copies, l_copies = [], [[] for _ in range(halves)], []
    logw_parts = []

    def over_tiles(j0, j1, body, carry):
        step = max(u for u in range(1, 8) if (j1 - j0) % u == 0)

        def several(i, carry):
            for u in range(step):
                carry = body(j0 + i * step + u, carry)
            return carry

        return lax.fori_loop(0, (j1 - j0) // step, several, carry)

    def bias_block(jp, h, g0, size):
        j0, j1 = span[jp]
        start = h * half + g0

        def add(j, total):
            return total + lax.dot_general(
                tiles_v[j], chol_v[j, start : start + size, :], NT_DIMS,
                preferred_element_type=F32,
            )

        total = bias_acc[:, start : start + size] if jp else jnp.zeros((wall, size), F32)
        total = over_tiles(j0, j1, add, total)
        if jp < parts - 1:
            bias_acc[:, start : start + size] = total
            return
        for k in range(size // chunk):
            kk = g0 // chunk + k
            part[h, kk] = total[:, k * chunk : (k + 1) * chunk]
            for wg in range(n // nch):
                d = wg * nch + kk
                copy = send(
                    part.at[h, kk, wg * wrows : (wg + 1) * wrows], part_got.at[h, me],
                    r_send.at[h, d], r_recv.at[h, me], d,
                )
                r_copies.append((d, copy))
                pl.when(me != d)(copy.start)

                @pl.when(me == d)
                def _():
                    part_got[h, me] = part[h, kk, wg * wrows : (wg + 1) * wrows]

    def reduce_bias(h):
        for src in others:
            send(
                part.at[h, 0, 0:wrows], part_got.at[h, src], r_send.at[h, src],
                r_recv.at[h, src], src,
            ).wait_recv()
        bias = part_got[h, 0]
        for s in range(1, n):
            bias = bias + part_got[h, s]
        drawn = jnp.zeros((wrows, chunk), jnp.int32)
        kind = jnp.zeros((1, chunk), jnp.int32)
        for d in range(n):
            g0 = h * half + (d % nch) * chunk
            w0 = (d // nch) * wrows
            drawn = jnp.where(me == d, aux_ref[w0 : w0 + wrows, g0 : g0 + chunk], drawn)
            kind = jnp.where(me == d, cgroup_ref[:, g0 : g0 + chunk], kind)
        weight = jnp.zeros((1, chunk), F32)
        for k in range(gweight_ref.shape[0]):
            weight = jnp.where(kind == k, gweight_ref[k], weight)
        sampled = drawn.astype(F32) * (1.0 / 262144.0)
        field_own[h] = (weight * (sampled - bias)).astype(BF).astype(F32)
        for i, dst in enumerate(others):
            copy = send(
                field_own.at[h], field_got.at[h, me], f_send.at[h, i], f_recv.at[h, i], dst
            )
            copy.start()
            f_copies[h].append(copy)
        field_got[h, me] = field_own[h]
        logw_parts.append(
            jnp.sum(sampled * bias - 0.5 * bias * bias, axis=1, keepdims=True)
        )

    def gather_fields(h):
        for copy in f_copies[h]:
            copy.wait_recv()
        for s in range(n):
            g0 = h * half + (s % nch) * chunk
            w0 = (s // nch) * wrows
            field_all[w0 : w0 + wrows, g0 : g0 + chunk] = field_got[h, s]
        fields_v[h] = field_all[:, h * half : (h + 1) * half].astype(BF)

    for jp in range(parts):
        for copy in a_copies[jp]:
            copy.wait_recv()
        j0 = jp * part_size
        tiles_v[j0 : j0 + part_size] = dot(
            swap_matrix(part_size, wall), got[jp].reshape(rows, entries)
        ).astype(BF).reshape(part_size, wall, entries)
        for h in range(halves):
            chol_copies[jp, h].wait()
            if jp == parts - 1 and h > 0:
                bias_block(jp, h, 0, half // 2)
                reduce_bias(h - 1)
                bias_block(jp, h, half // 2, half // 2)
            else:
                bias_block(jp, h, 0, half)

    gather_fields(0)
    for h in range(halves - 1):
        for jp, (j0, j1) in enumerate(span):
            def spread(j, carry):
                new = dot(fields_v[h], chol_v[j, h * half : (h + 1) * half, :])
                pot_acc[j] = new if h == 0 else pot_acc[j] + new
                return carry

            over_tiles(j0, j1, spread, 0)
            if jp == 0 and h == halves - 2:
                reduce_bias(halves - 1)
        gather_fields(h + 1)
    b_copies = [[] for _ in range(parts)]
    h = halves - 1
    for jp, (j0, j1) in enumerate(span):
        def finish(j, carry):
            pot_v[j] = (
                pot_acc[j] + dot(fields_v[h], chol_v[j, h * half : (h + 1) * half, :])
            ).astype(BF)
            return carry

        over_tiles(j0, j1, finish, 0)
        for j in range(j1, j0 + part_size):
            pot_v[j] = jnp.zeros((wall, entries), BF)
        back[jp] = dot(
            swap_matrix(wall, part_size), pot_v[j0 : j0 + part_size].reshape(rows, entries)
        ).astype(BF).reshape(n, part_size, entries)
        for i, dst in enumerate(others):
            copy = send(
                back.at[jp, dst], back_got.at[jp, me], b_send.at[jp, i], b_recv.at[jp, i], dst
            )
            copy.start()
            b_copies[jp].append(copy)
        back_got[jp, me] = back[jp, me]

    logw = sum(logw_parts[1:], logw_parts[0])
    logw_own[...] = jnp.broadcast_to(logw, logw_own.shape)
    for off in range(1, nch):
        dst = me - mine_k + lax.rem(mine_k + off, nch)
        copy = send(logw_own, logw_got.at[mine_k], l_send.at[off], l_recv.at[off], dst)
        copy.start()
        l_copies.append(copy)
    logw_got[mine_k] = logw_own[...]
    unperm = swap_matrix(NBLK, side)
    gather = [hot(iota((ntile, rows), 0) == lane_tile[jp]) for jp in range(parts)]

    pot_t = jnp.zeros((ntile, entries), F32)
    for jp in range(parts):
        for copy in b_copies[jp]:
            copy.wait_recv()
        pot_t = pot_t + dot(gather[jp], back_got[jp].reshape(rows, entries))
    wide = dot(pot_t.astype(BF), spots[...]).astype(BF) * col_mask
    placed = dot(put, wide).astype(BF)
    for p in range(side):
        for c in range(ngroup):
            v_mat[p * NBLK : (p + 1) * NBLK, c * chunk : (c + 1) * chunk] = placed[
                c * NBLK : (c + 1) * NBLK, p * chunk : (p + 1) * chunk
            ]
    v_mat[...] = dot(unperm, v_mat[...]).astype(BF)
    term_v[...] = walk_ref[0]
    running_v[...] = walk_ref[0].astype(F32)

    def taylor(degree, carry):
        term = (dot(v_mat[...], term_v[...]) / degree.astype(F32)).astype(BF)
        term_v[...] = term
        running_v[...] = running_v[...] + term.astype(F32)
        return carry

    lax.fori_loop(1, 5, taylor, 0)
    adv_ref[0] = running_v[...].astype(BF)

    for copy in l_copies:
        copy.wait_recv()
    logw = logw_got[0]
    for s in range(1, nch):
        logw = logw + logw_got[s]
    mine = (iota(logw.shape, 0) == lax.rem(me, wrows)) & (iota(logw.shape, 1) == 0)
    lw_ref[0] = jnp.sum(jnp.where(mine, logw, 0.0))
    for copy in sum(a_copies + f_copies + b_copies, l_copies):
        copy.wait_send()
    for d, copy in r_copies:
        pl.when(me != d)(copy.wait_send)


def per_device(
    walkers, green_factor, trial, chol, pattern, owner_counts, chol_group, group_weight, aux
):
    n = owner_counts.shape[0]
    cap, nchol, entries = chol.shape
    wall = aux.shape[0]
    assert walkers.shape[0] == 1 and wall == n
    orbitals = walkers.shape[1]
    chunk, part_size, halves = 128, 16, 2
    nch = nchol // halves // chunk
    assert n % nch == 0
    parts = -(-cap // part_size)
    side = orbitals // NBLK
    wrows = wall * nch // n
    dma = pltpu.SemaphoreType.DMA
    vmem = pl.BlockSpec(memory_space=pltpu.VMEM)
    smem = pl.BlockSpec(memory_space=pltpu.SMEM)
    advanced, log_weight = pl.pallas_call(
        functools.partial(kernel, n, cap, part_size, halves, chunk),
        out_shape=(
            jax.ShapeDtypeStruct(walkers.shape, BF),
            jax.ShapeDtypeStruct((1,), F32),
        ),
        in_specs=[vmem, vmem, vmem, pl.BlockSpec(memory_space=pl.ANY), vmem, smem, vmem, smem, vmem],
        out_specs=(vmem, smem),
        scratch_shapes=[
            pltpu.VMEM((cap, nchol, entries), BF),
            pltpu.VMEM((entries, side * chunk), BF),
            pltpu.VMEM((orbitals // chunk * NBLK, side * chunk), BF),
            pltpu.VMEM((parts, n, part_size, entries), BF),
            pltpu.VMEM((parts, n, part_size, entries), BF),
            pltpu.VMEM((parts * part_size, wall, entries), BF),
            pltpu.VMEM((wall, nchol), F32),
            pltpu.VMEM((halves, nch, wall, chunk), F32),
            pltpu.VMEM((halves, n, wrows, chunk), F32),
            pltpu.VMEM((halves, wrows, chunk), F32),
            pltpu.VMEM((halves, n, wrows, chunk), F32),
            pltpu.VMEM((wall, nchol), F32),
            pltpu.VMEM((halves, wall, nchol // halves), BF),
            pltpu.VMEM((wrows, chunk), F32),
            pltpu.VMEM((nch, wrows, chunk), F32),
            pltpu.VMEM((cap, wall, entries), F32),
            pltpu.VMEM((parts * part_size, wall, entries), BF),
            pltpu.VMEM((parts, n, part_size, entries), BF),
            pltpu.VMEM((parts, n, part_size, entries), BF),
            pltpu.VMEM((orbitals, orbitals), BF),
            pltpu.VMEM(walkers.shape[1:], BF),
            pltpu.VMEM(walkers.shape[1:], F32),
            dma((parts, halves)),
            dma((parts, n)), dma((parts, n)),
            dma((halves, n)), dma((halves, n)),
            dma((halves, n)), dma((halves, n)),
            dma((nch,)), dma((nch,)),
            dma((parts, n)), dma((parts, n)),
        ],
        compiler_params=pltpu.CompilerParams(
            collective_id=0, has_side_effects=True, vmem_limit_bytes=56 * 2**20
        ),
        cost_estimate=pl.CostEstimate(
            flops=4 * wall * cap * nchol * entries, bytes_accessed=2 * chol.size, transcendentals=0
        ),
    )(
        walkers, green_factor, trial, chol, pattern.reshape(1, -1), owner_counts,
        chol_group.reshape(1, -1), group_weight, aux,
    )
    return advanced, log_weight


def solution(mesh):
    return jax.shard_map(
        per_device,
        mesh=mesh,
        in_specs=(
            P(("groups", "tile"), None, None),
            P(("groups", "tile"), None, None),
            P(),
            P("tile", None, None),
            P(),
            P(),
            P(),
            P(),
            P("groups", None),
        ),
        out_specs=(P(("groups", "tile"), None, None), P(("groups", "tile"))),
        check_vma=False,
    )
```

```python
import functools

import jax
import jax.numpy as jnp
from jax import lax
from jax.experimental import pallas as pl
from jax.experimental.pallas import tpu as pltpu
from jax.sharding import PartitionSpec as P

NBLK = 32
BF = jnp.bfloat16
F32 = jnp.float32
NT_DIMS = (((1,), (1,)), ((), ()))


def quot(x, k):
    if k & (k - 1) == 0:
        return lax.shift_right_logical(x, jnp.int32(k.bit_length() - 1))
    return lax.div(x, jnp.int32(k))


def mod(x, k):
    if k & (k - 1) == 0:
        return lax.bitwise_and(x, jnp.int32(k - 1))
    return lax.rem(x, jnp.int32(k))


def iota(shape, dim):
    return lax.broadcasted_iota(jnp.int32, shape, dim)


def hot(cond):
    return jnp.where(cond, 1.0, 0.0).astype(BF)


def dot(a, b):
    return jnp.dot(a, b, preferred_element_type=F32)


def swap_matrix(outer, inner):
    size = outer * inner
    row = iota((size, size), 0)
    col = iota((size, size), 1)
    return hot(col == mod(row, inner) * outer + quot(row, inner))


def kernel(
    n, cap, part_size, halves, chunk,
    walk_ref, factor_ref, trial_ref, chol_ref, pattern_ref, counts_ref, cgroup_ref, gweight_ref,
    aux_ref,
    adv_ref, lw_ref,
    chol_v, spots, green_v, sent, got, tiles_v, bias_acc, part, part_got, field_own, field_got,
    field_all, fields_v, logw_own, logw_got, pot_acc, pot_v, back, back_got, v_mat, term_v, running_v,
    chol_sem, a_send, a_recv, r_send, r_recv, f_send, f_recv, l_send, l_recv, b_send, b_recv,
):
    me = lax.axis_index("tile")
    orbitals = walk_ref.shape[1]
    nchol, entries = chol_ref.shape[1], chol_ref.shape[2]
    ntile = pattern_ref.shape[1]
    wall = aux_ref.shape[0]
    side = orbitals // NBLK
    group = chunk // side
    ngroup = NBLK // group
    half = nchol // halves
    nch = half // chunk
    wrows = wall * nch // n
    parts = -(-cap // part_size)
    rows = n * part_size
    mine_k = lax.rem(me, nch)
    others = [lax.rem(me + off, n) for off in range(1, n)]

    def send(src, dst, ssem, rsem, dev):
        return pltpu.make_async_remote_copy(
            src_ref=src, dst_ref=dst, send_sem=ssem, recv_sem=rsem,
            device_id={"tile": dev}, device_id_type=pl.DeviceIdType.MESH,
        )

    def received(ref, sem):
        send(ref, ref, sem, sem, others[0]).wait_recv()

    def sent_out(ref, sem):
        send(ref, ref, sem, sem, others[0]).wait_send()

    barrier = pltpu.get_barrier_semaphore()
    for dst in others:
        pl.semaphore_signal(
            barrier, inc=1, device_id={"tile": dst}, device_id_type=pl.DeviceIdType.MESH
        )
    span = [(jp * part_size, min(cap, (jp + 1) * part_size)) for jp in range(parts)]
    chol_copies = {}
    for jp, (j0, j1) in enumerate(span):
        for h in range(halves):
            piece = (pl.ds(j0, j1 - j0), pl.ds(h * half, half), slice(None))
            chol_copies[jp, h] = pltpu.make_async_copy(
                chol_ref.at[piece], chol_v.at[piece], chol_sem.at[jp, h]
            )
            if jp == 0:
                chol_copies[jp, h].start()

    perm = swap_matrix(side, NBLK)
    factor = dot(perm, factor_ref[0]).astype(BF)
    green = lax.dot_general(
        factor, trial_ref[...], NT_DIMS, preferred_element_type=F32
    ).astype(BF)
    for p in range(side):
        for c in range(ngroup):
            green_v[c * NBLK : (c + 1) * NBLK, p * chunk : (p + 1) * chunk] = green[
                p * NBLK : (p + 1) * NBLK, c * chunk : (c + 1) * chunk
            ]
    pat_row = pattern_ref[...]
    pat_col = jnp.transpose(jnp.broadcast_to(pat_row, (128, ntile)))[:, :1]

    def place(pat):
        return quot(mod(pat, NBLK), group) * NBLK + quot(pat, NBLK)

    pick = hot(place(pat_col) == iota((ntile, ngroup * NBLK), 1))
    put = hot(place(pat_row) == iota((ngroup * NBLK, ntile), 0))
    col_mask = hot(mod(pat_col, group) == quot(iota((ntile, chunk), 1), side))
    col_mask = jnp.concatenate([col_mask] * side, axis=1)
    wide_lane = iota((entries, side * chunk), 1)
    spots[...] = hot(
        iota((entries, side * chunk), 0) == quot(wide_lane, chunk) * side + mod(wide_lane, side)
    )
    chosen = dot(pick, green_v[...]).astype(BF) * col_mask
    green_t = lax.dot_general(chosen, spots[...], NT_DIMS, preferred_element_type=F32).astype(BF)

    first = jnp.int32(0)
    lane = iota((1, rows), 1)
    slot = iota((part_size, ntile), 0)
    tile_lane = iota((part_size, ntile), 1)
    lane_tile = [jnp.full((1, rows), -1, jnp.int32) for _ in range(parts)]
    own = [[] for _ in range(parts)]
    for d in range(n):
        held = counts_ref[d]
        for jp in range(parts):
            at = slot + jp * part_size
            own[jp].append(jnp.where((tile_lane == at + first) & (at < held), 1.0, 0.0))
            in_part = lane - d * part_size
            at = in_part + jp * part_size
            live = (in_part >= 0) & (in_part < part_size) & (at < held)
            lane_tile[jp] = jnp.where(live, at + first, lane_tile[jp])
        first = first + held

    for jp in range(parts):
        rows_out = dot(jnp.concatenate(own[jp], axis=0).astype(BF), green_t)
        sent[jp] = rows_out.astype(BF).reshape(n, part_size, entries)
        if jp == 0:
            pl.semaphore_wait(barrier, n - 1)
        for dst in others:
            send(sent.at[jp, dst], got.at[jp, me], a_send.at[jp], a_recv.at[jp], dst).start()
        if jp + 1 < parts:
            for h in range(halves):
                chol_copies[jp + 1, h].start()
        got[jp, me] = sent[jp, me]

    logw_parts = []

    def over_tiles(j0, j1, body, carry):
        step = max(u for u in range(1, 8) if (j1 - j0) % u == 0)

        def several(i, carry):
            for u in range(step):
                carry = body(j0 + i * step + u, carry)
            return carry

        return lax.fori_loop(0, (j1 - j0) // step, several, carry)

    def bias_block(jp, h, g0, size):
        j0, j1 = span[jp]
        start = h * half + g0

        def add(j, total):
            return total + lax.dot_general(
                tiles_v[j], chol_v[j, start : start + size, :], NT_DIMS,
                preferred_element_type=F32,
            )

        total = bias_acc[:, start : start + size] if jp else jnp.zeros((wall, size), F32)
        total = over_tiles(j0, j1, add, total)
        if jp < parts - 1:
            bias_acc[:, start : start + size] = total
            return
        for k in range(size // chunk):
            for wg in range(n // nch):
                part[h, wg * nch + g0 // chunk + k] = total[
                    wg * wrows : (wg + 1) * wrows, k * chunk : (k + 1) * chunk
                ]
        if g0 + size == half:
            for dst in others:
                send(
                    part.at[h, dst], part_got.at[h, me], r_send.at[h], r_recv.at[h], dst
                ).start()
            part_got[h, me] = part[h, me]

    def reduce_bias(h):
        received(part_got.at[h, 0 : n - 1], r_recv.at[h])
        bias = part_got[h, 0]
        for s in range(1, n):
            bias = bias + part_got[h, s]
        drawn = jnp.zeros((wrows, chunk), jnp.int32)
        kind = jnp.zeros((1, chunk), jnp.int32)
        for d in range(n):
            g0 = h * half + (d % nch) * chunk
            w0 = (d // nch) * wrows
            drawn = jnp.where(me == d, aux_ref[w0 : w0 + wrows, g0 : g0 + chunk], drawn)
            kind = jnp.where(me == d, cgroup_ref[:, g0 : g0 + chunk], kind)
        weight = jnp.zeros((1, chunk), F32)
        for k in range(gweight_ref.shape[0]):
            weight = jnp.where(kind == k, gweight_ref[k], weight)
        sampled = drawn.astype(F32) * (1.0 / 262144.0)
        field_own[h] = (weight * (sampled - bias)).astype(BF).astype(F32)
        for dst in others:
            send(
                field_own.at[h], field_got.at[h, me], f_send.at[h], f_recv.at[h], dst
            ).start()
        field_got[h, me] = field_own[h]
        logw_parts.append(
            jnp.sum(sampled * bias - 0.5 * bias * bias, axis=1, keepdims=True)
        )

    def gather_fields(h):
        received(field_got.at[h, 0 : n - 1], f_recv.at[h])
        for s in range(n):
            g0 = h * half + (s % nch) * chunk
            w0 = (s // nch) * wrows
            field_all[w0 : w0 + wrows, g0 : g0 + chunk] = field_got[h, s]
        fields_v[h] = field_all[:, h * half : (h + 1) * half].astype(BF)

    for jp in range(parts):
        received(got.at[jp, 0 : n - 1], a_recv.at[jp])
        j0 = jp * part_size
        tiles_v[j0 : j0 + part_size] = dot(
            swap_matrix(part_size, wall), got[jp].reshape(rows, entries)
        ).astype(BF).reshape(part_size, wall, entries)
        for h in range(halves):
            chol_copies[jp, h].wait()
            if jp == parts - 1 and h > 0:
                bias_block(jp, h, 0, half // 2)
                reduce_bias(h - 1)
                bias_block(jp, h, half // 2, half // 2)
            else:
                bias_block(jp, h, 0, half)

    gather_fields(0)
    for h in range(halves - 1):
        for jp, (j0, j1) in enumerate(span):
            def spread(j, carry):
                new = dot(fields_v[h], chol_v[j, h * half : (h + 1) * half, :])
                pot_acc[j] = new if h == 0 else pot_acc[j] + new
                return carry

            over_tiles(j0, j1, spread, 0)
            if jp == 0 and h == halves - 2:
                reduce_bias(halves - 1)
        gather_fields(h + 1)
    h = halves - 1
    for jp, (j0, j1) in enumerate(span):
        def finish(j, carry):
            pot_v[j] = (
                pot_acc[j] + dot(fields_v[h], chol_v[j, h * half : (h + 1) * half, :])
            ).astype(BF)
            return carry

        over_tiles(j0, j1, finish, 0)
        for j in range(j1, j0 + part_size):
            pot_v[j] = jnp.zeros((wall, entries), BF)
        back[jp] = dot(
            swap_matrix(wall, part_size), pot_v[j0 : j0 + part_size].reshape(rows, entries)
        ).astype(BF).reshape(n, part_size, entries)
        for dst in others:
            send(
                back.at[jp, dst], back_got.at[jp, me], b_send.at[jp], b_recv.at[jp], dst
            ).start()
        back_got[jp, me] = back[jp, me]

    logw = sum(logw_parts[1:], logw_parts[0])
    logw_own[...] = jnp.broadcast_to(logw, logw_own.shape)
    for off in range(1, nch):
        dst = me - mine_k + lax.rem(mine_k + off, nch)
        send(logw_own, logw_got.at[mine_k], l_send, l_recv, dst).start()
    logw_got[mine_k] = logw_own[...]
    unperm = swap_matrix(NBLK, side)
    gather = [hot(iota((ntile, rows), 0) == lane_tile[jp]) for jp in range(parts)]

    for h in range(halves):
        sent_out(part_got.at[h, 0 : n - 1], r_send.at[h])
        sent_out(field_got.at[h, 0 : n - 1], f_send.at[h])
    for jp in range(parts):
        sent_out(got.at[jp, 0 : n - 1], a_send.at[jp])

    pot_t = jnp.zeros((ntile, entries), F32)
    for jp in range(parts):
        received(back_got.at[jp, 0 : n - 1], b_recv.at[jp])
        pot_t = pot_t + dot(gather[jp], back_got[jp].reshape(rows, entries))
    wide = dot(pot_t.astype(BF), spots[...]).astype(BF) * col_mask
    placed = dot(put, wide).astype(BF)
    for p in range(side):
        for c in range(ngroup):
            v_mat[p * NBLK : (p + 1) * NBLK, c * chunk : (c + 1) * chunk] = placed[
                c * NBLK : (c + 1) * NBLK, p * chunk : (p + 1) * chunk
            ]
    v_mat[...] = dot(unperm, v_mat[...]).astype(BF)
    term_v[...] = walk_ref[0]
    running_v[...] = walk_ref[0].astype(F32)

    def taylor(degree, carry):
        term = (dot(v_mat[...], term_v[...]) / degree.astype(F32)).astype(BF)
        term_v[...] = term
        running_v[...] = running_v[...] + term.astype(F32)
        return carry

    lax.fori_loop(1, 5, taylor, 0)
    adv_ref[0] = running_v[...].astype(BF)

    received(logw_got.at[0 : nch - 1], l_recv)
    logw = logw_got[0]
    for s in range(1, nch):
        logw = logw + logw_got[s]
    mine = (iota(logw.shape, 0) == lax.rem(me, wrows)) & (iota(logw.shape, 1) == 0)
    lw_ref[0] = jnp.sum(jnp.where(mine, logw, 0.0))
    sent_out(logw_got.at[0 : nch - 1], l_send)
    for jp in range(parts):
        sent_out(back_got.at[jp, 0 : n - 1], b_send.at[jp])


def per_device(
    walkers, green_factor, trial, chol, pattern, owner_counts, chol_group, group_weight, aux
):
    n = owner_counts.shape[0]
    cap, nchol, entries = chol.shape
    wall = aux.shape[0]
    assert walkers.shape[0] == 1 and wall == n
    orbitals = walkers.shape[1]
    chunk, part_size, halves = 128, 16, 2
    nch = nchol // halves // chunk
    assert n % nch == 0
    parts = -(-cap // part_size)
    side = orbitals // NBLK
    wrows = wall * nch // n
    dma = pltpu.SemaphoreType.DMA
    vmem = pl.BlockSpec(memory_space=pltpu.VMEM)
    smem = pl.BlockSpec(memory_space=pltpu.SMEM)
    advanced, log_weight = pl.pallas_call(
        functools.partial(kernel, n, cap, part_size, halves, chunk),
        out_shape=(
            jax.ShapeDtypeStruct(walkers.shape, BF),
            jax.ShapeDtypeStruct((1,), F32),
        ),
        in_specs=[vmem, vmem, vmem, pl.BlockSpec(memory_space=pl.ANY), vmem, smem, vmem, smem, vmem],
        out_specs=(vmem, smem),
        scratch_shapes=[
            pltpu.VMEM((cap, nchol, entries), BF),
            pltpu.VMEM((entries, side * chunk), BF),
            pltpu.VMEM((orbitals // chunk * NBLK, side * chunk), BF),
            pltpu.VMEM((parts, n, part_size, entries), BF),
            pltpu.VMEM((parts, n, part_size, entries), BF),
            pltpu.VMEM((parts * part_size, wall, entries), BF),
            pltpu.VMEM((wall, nchol), F32),
            pltpu.VMEM((halves, n, wrows, chunk), F32),
            pltpu.VMEM((halves, n, wrows, chunk), F32),
            pltpu.VMEM((halves, wrows, chunk), F32),
            pltpu.VMEM((halves, n, wrows, chunk), F32),
            pltpu.VMEM((wall, nchol), F32),
            pltpu.VMEM((halves, wall, nchol // halves), BF),
            pltpu.VMEM((wrows, chunk), F32),
            pltpu.VMEM((nch, wrows, chunk), F32),
            pltpu.VMEM((cap, wall, entries), F32),
            pltpu.VMEM((parts * part_size, wall, entries), BF),
            pltpu.VMEM((parts, n, part_size, entries), BF),
            pltpu.VMEM((parts, n, part_size, entries), BF),
            pltpu.VMEM((orbitals, orbitals), BF),
            pltpu.VMEM(walkers.shape[1:], BF),
            pltpu.VMEM(walkers.shape[1:], F32),
            dma((parts, halves)),
            dma((parts,)), dma((parts,)),
            dma((halves,)), dma((halves,)),
            dma((halves,)), dma((halves,)),
            dma, dma,
            dma((parts,)), dma((parts,)),
        ],
        compiler_params=pltpu.CompilerParams(
            collective_id=0, has_side_effects=True, vmem_limit_bytes=56 * 2**20
        ),
        cost_estimate=pl.CostEstimate(
            flops=4 * wall * cap * nchol * entries, bytes_accessed=2 * chol.size, transcendentals=0
        ),
    )(
        walkers, green_factor, trial, chol, pattern.reshape(1, -1), owner_counts,
        chol_group.reshape(1, -1), group_weight, aux,
    )
    return advanced, log_weight


def solution(mesh):
    return jax.shard_map(
        per_device,
        mesh=mesh,
        in_specs=(
            P(("groups", "tile"), None, None),
            P(("groups", "tile"), None, None),
            P(),
            P("tile", None, None),
            P(),
            P(),
            P(),
            P(),
            P("groups", None),
        ),
        out_specs=(P(("groups", "tile"), None, None), P(("groups", "tile"))),
        check_vma=False,
    )
```

```python
import functools

import jax
import jax.numpy as jnp
from jax import lax
from jax.experimental import pallas as pl
from jax.experimental.pallas import tpu as pltpu
from jax.sharding import PartitionSpec as P

NBLK = 32
BF = jnp.bfloat16
F32 = jnp.float32
NT_DIMS = (((1,), (1,)), ((), ()))


def quot(x, k):
    if k & (k - 1) == 0:
        return lax.shift_right_logical(x, jnp.int32(k.bit_length() - 1))
    return lax.div(x, jnp.int32(k))


def mod(x, k):
    if k & (k - 1) == 0:
        return lax.bitwise_and(x, jnp.int32(k - 1))
    return lax.rem(x, jnp.int32(k))


def iota(shape, dim):
    return lax.broadcasted_iota(jnp.int32, shape, dim)


def hot(cond):
    return jnp.where(cond, 1.0, 0.0).astype(BF)


def dot(a, b):
    return jnp.dot(a, b, preferred_element_type=F32)


def swap_matrix(outer, inner):
    size = outer * inner
    row = iota((size, size), 0)
    col = iota((size, size), 1)
    return hot(col == mod(row, inner) * outer + quot(row, inner))


def kernel(
    n, cap, part_size, halves, chunk,
    walk_hbm, factor_hbm, trial_hbm, chol_ref, pattern_ref, counts_ref, cgroup_ref, gweight_ref,
    aux_hbm,
    adv_ref, lw_ref,
    walk_ref, factor_ref, trial_ref, aux_ref, chol_v, spots, green_v, sent, got, tiles_v, bias_acc, part, part_got, field_own, field_got,
    field_all, fields_v, logw_own, logw_got, pot_acc, pot_v, back, back_got, v_mat, term_v, running_v,
    in_sem, chol_sem, a_send, a_recv, r_send, r_recv, f_send, f_recv, l_send, l_recv, b_send, b_recv,
):
    me = lax.axis_index("tile")
    orbitals = walk_ref.shape[1]
    nchol, entries = chol_ref.shape[1], chol_ref.shape[2]
    ntile = pattern_ref.shape[1]
    wall = aux_ref.shape[0]
    side = orbitals // NBLK
    group = chunk // side
    ngroup = NBLK // group
    half = nchol // halves
    nch = half // chunk
    wrows = wall * nch // n
    parts = -(-cap // part_size)
    rows = n * part_size
    mine_k = lax.rem(me, nch)
    others = [lax.rem(me + off, n) for off in range(1, n)]

    def send(src, dst, ssem, rsem, dev):
        return pltpu.make_async_remote_copy(
            src_ref=src, dst_ref=dst, send_sem=ssem, recv_sem=rsem,
            device_id={"tile": dev}, device_id_type=pl.DeviceIdType.MESH,
        )

    def received(ref, sem):
        send(ref, ref, sem, sem, others[0]).wait_recv()

    def sent_out(ref, sem):
        send(ref, ref, sem, sem, others[0]).wait_send()

    barrier = pltpu.get_barrier_semaphore()
    for dst in others:
        pl.semaphore_signal(
            barrier, inc=1, device_id={"tile": dst}, device_id_type=pl.DeviceIdType.MESH
        )
    in_copies = [
        pltpu.make_async_copy(src, dst, in_sem.at[i])
        for i, (src, dst) in enumerate(
            (
                (factor_hbm, factor_ref),
                (trial_hbm, trial_ref),
                (walk_hbm, walk_ref),
                (aux_hbm, aux_ref),
            )
        )
    ]
    for copy in in_copies:
        copy.start()
    span = [(jp * part_size, min(cap, (jp + 1) * part_size)) for jp in range(parts)]
    chol_copies = {}
    for jp, (j0, j1) in enumerate(span):
        for h in range(halves):
            piece = (pl.ds(j0, j1 - j0), pl.ds(h * half, half), slice(None))
            chol_copies[jp, h] = pltpu.make_async_copy(
                chol_ref.at[piece], chol_v.at[piece], chol_sem.at[jp, h]
            )
            if jp == 0:
                chol_copies[jp, h].start()

    perm = swap_matrix(side, NBLK)
    in_copies[0].wait()
    factor = dot(perm, factor_ref[0]).astype(BF)
    in_copies[1].wait()
    green = lax.dot_general(
        factor, trial_ref[...], NT_DIMS, preferred_element_type=F32
    ).astype(BF)
    for p in range(side):
        for c in range(ngroup):
            green_v[c * NBLK : (c + 1) * NBLK, p * chunk : (p + 1) * chunk] = green[
                p * NBLK : (p + 1) * NBLK, c * chunk : (c + 1) * chunk
            ]
    pat_row = pattern_ref[...]
    pat_col = jnp.transpose(jnp.broadcast_to(pat_row, (128, ntile)))[:, :1]

    def place(pat):
        return quot(mod(pat, NBLK), group) * NBLK + quot(pat, NBLK)

    pick = hot(place(pat_col) == iota((ntile, ngroup * NBLK), 1))
    put = hot(place(pat_row) == iota((ngroup * NBLK, ntile), 0))
    col_mask = hot(mod(pat_col, group) == quot(iota((ntile, chunk), 1), side))
    col_mask = jnp.concatenate([col_mask] * side, axis=1)
    wide_lane = iota((entries, side * chunk), 1)
    spots[...] = hot(
        iota((entries, side * chunk), 0) == quot(wide_lane, chunk) * side + mod(wide_lane, side)
    )
    chosen = dot(pick, green_v[...]).astype(BF) * col_mask
    green_t = lax.dot_general(chosen, spots[...], NT_DIMS, preferred_element_type=F32).astype(BF)

    first = jnp.int32(0)
    lane = iota((1, rows), 1)
    slot = iota((part_size, ntile), 0)
    tile_lane = iota((part_size, ntile), 1)
    lane_tile = [jnp.full((1, rows), -1, jnp.int32) for _ in range(parts)]
    own = [[] for _ in range(parts)]
    for d in range(n):
        held = counts_ref[d]
        for jp in range(parts):
            at = slot + jp * part_size
            own[jp].append(jnp.where((tile_lane == at + first) & (at < held), 1.0, 0.0))
            in_part = lane - d * part_size
            at = in_part + jp * part_size
            live = (in_part >= 0) & (in_part < part_size) & (at < held)
            lane_tile[jp] = jnp.where(live, at + first, lane_tile[jp])
        first = first + held

    for jp in range(parts):
        rows_out = dot(jnp.concatenate(own[jp], axis=0).astype(BF), green_t)
        sent[jp] = rows_out.astype(BF).reshape(n, part_size, entries)
        if jp == 0:
            pl.semaphore_wait(barrier, n - 1)
        for dst in others:
            send(sent.at[jp, dst], got.at[jp, me], a_send.at[jp], a_recv.at[jp], dst).start()
        if jp + 1 < parts:
            for h in range(halves):
                chol_copies[jp + 1, h].start()
        got[jp, me] = sent[jp, me]

    for copy in in_copies[2:]:
        copy.wait()
    logw_parts = []

    def over_tiles(j0, j1, body, carry):
        step = max(u for u in range(1, 8) if (j1 - j0) % u == 0)

        def several(i, carry):
            for u in range(step):
                carry = body(j0 + i * step + u, carry)
            return carry

        return lax.fori_loop(0, (j1 - j0) // step, several, carry)

    def bias_block(jp, h, g0, size):
        j0, j1 = span[jp]
        start = h * half + g0

        def add(j, total):
            return total + lax.dot_general(
                tiles_v[j], chol_v[j, start : start + size, :], NT_DIMS,
                preferred_element_type=F32,
            )

        total = bias_acc[:, start : start + size] if jp else jnp.zeros((wall, size), F32)
        total = over_tiles(j0, j1, add, total)
        if jp < parts - 1:
            bias_acc[:, start : start + size] = total
            return
        for k in range(size // chunk):
            for wg in range(n // nch):
                part[h, wg * nch + g0 // chunk + k] = total[
                    wg * wrows : (wg + 1) * wrows, k * chunk : (k + 1) * chunk
                ]
        if g0 + size == half:
            for dst in others:
                send(
                    part.at[h, dst], part_got.at[h, me], r_send.at[h], r_recv.at[h], dst
                ).start()
            part_got[h, me] = part[h, me]

    def reduce_bias(h):
        received(part_got.at[h, 0 : n - 1], r_recv.at[h])
        bias = part_got[h, 0]
        for s in range(1, n):
            bias = bias + part_got[h, s]
        drawn = jnp.zeros((wrows, chunk), jnp.int32)
        kind = jnp.zeros((1, chunk), jnp.int32)
        for d in range(n):
            g0 = h * half + (d % nch) * chunk
            w0 = (d // nch) * wrows
            drawn = jnp.where(me == d, aux_ref[w0 : w0 + wrows, g0 : g0 + chunk], drawn)
            kind = jnp.where(me == d, cgroup_ref[:, g0 : g0 + chunk], kind)
        weight = jnp.zeros((1, chunk), F32)
        for k in range(gweight_ref.shape[0]):
            weight = jnp.where(kind == k, gweight_ref[k], weight)
        sampled = drawn.astype(F32) * (1.0 / 262144.0)
        field_own[h] = (weight * (sampled - bias)).astype(BF).astype(F32)
        for dst in others:
            send(
                field_own.at[h], field_got.at[h, me], f_send.at[h], f_recv.at[h], dst
            ).start()
        field_got[h, me] = field_own[h]
        logw_parts.append(
            jnp.sum(sampled * bias - 0.5 * bias * bias, axis=1, keepdims=True)
        )

    def gather_fields(h):
        received(field_got.at[h, 0 : n - 1], f_recv.at[h])
        for s in range(n):
            g0 = h * half + (s % nch) * chunk
            w0 = (s // nch) * wrows
            field_all[w0 : w0 + wrows, g0 : g0 + chunk] = field_got[h, s]
        fields_v[h] = field_all[:, h * half : (h + 1) * half].astype(BF)

    for jp in range(parts):
        received(got.at[jp, 0 : n - 1], a_recv.at[jp])
        j0 = jp * part_size
        tiles_v[j0 : j0 + part_size] = dot(
            swap_matrix(part_size, wall), got[jp].reshape(rows, entries)
        ).astype(BF).reshape(part_size, wall, entries)
        for h in range(halves):
            chol_copies[jp, h].wait()
            if jp == parts - 1 and h > 0:
                bias_block(jp, h, 0, half // 2)
                reduce_bias(h - 1)
                bias_block(jp, h, half // 2, half // 2)
            else:
                bias_block(jp, h, 0, half)

    gather_fields(0)
    for h in range(halves - 1):
        for jp, (j0, j1) in enumerate(span):
            def spread(j, carry):
                new = dot(fields_v[h], chol_v[j, h * half : (h + 1) * half, :])
                pot_acc[j] = new if h == 0 else pot_acc[j] + new
                return carry

            over_tiles(j0, j1, spread, 0)
            if jp == 0 and h == halves - 2:
                reduce_bias(halves - 1)
        gather_fields(h + 1)
    h = halves - 1
    for jp, (j0, j1) in enumerate(span):
        def finish(j, carry):
            pot_v[j] = (
                pot_acc[j] + dot(fields_v[h], chol_v[j, h * half : (h + 1) * half, :])
            ).astype(BF)
            return carry

        over_tiles(j0, j1, finish, 0)
        for j in range(j1, j0 + part_size):
            pot_v[j] = jnp.zeros((wall, entries), BF)
        back[jp] = dot(
            swap_matrix(wall, part_size), pot_v[j0 : j0 + part_size].reshape(rows, entries)
        ).astype(BF).reshape(n, part_size, entries)
        for dst in others:
            send(
                back.at[jp, dst], back_got.at[jp, me], b_send.at[jp], b_recv.at[jp], dst
            ).start()
        back_got[jp, me] = back[jp, me]

    logw = sum(logw_parts[1:], logw_parts[0])
    logw_own[...] = jnp.broadcast_to(logw, logw_own.shape)
    for off in range(1, nch):
        dst = me - mine_k + lax.rem(mine_k + off, nch)
        send(logw_own, logw_got.at[mine_k], l_send, l_recv, dst).start()
    logw_got[mine_k] = logw_own[...]
    unperm = swap_matrix(NBLK, side)
    gather = [hot(iota((ntile, rows), 0) == lane_tile[jp]) for jp in range(parts)]

    for h in range(halves):
        sent_out(part_got.at[h, 0 : n - 1], r_send.at[h])
        sent_out(field_got.at[h, 0 : n - 1], f_send.at[h])
    for jp in range(parts):
        sent_out(got.at[jp, 0 : n - 1], a_send.at[jp])

    pot_t = jnp.zeros((ntile, entries), F32)
    for jp in range(parts):
        received(back_got.at[jp, 0 : n - 1], b_recv.at[jp])
        pot_t = pot_t + dot(gather[jp], back_got[jp].reshape(rows, entries))
    wide = dot(pot_t.astype(BF), spots[...]).astype(BF) * col_mask
    placed = dot(put, wide).astype(BF)
    for p in range(side):
        for c in range(ngroup):
            v_mat[p * NBLK : (p + 1) * NBLK, c * chunk : (c + 1) * chunk] = placed[
                c * NBLK : (c + 1) * NBLK, p * chunk : (p + 1) * chunk
            ]
    v_mat[...] = dot(unperm, v_mat[...]).astype(BF)
    term_v[...] = walk_ref[0]
    running_v[...] = walk_ref[0].astype(F32)

    def taylor(degree, carry):
        inverse = jnp.where(degree == 3, jnp.float32(1.0 / 3.0), jnp.float32(0.25))
        inverse = jnp.where(degree == 1, 1.0, jnp.where(degree == 2, 0.5, inverse))
        term = (dot(v_mat[...], term_v[...]) * inverse).astype(BF)
        term_v[...] = term
        running_v[...] = running_v[...] + term.astype(F32)
        return carry

    lax.fori_loop(1, 5, taylor, 0)
    adv_ref[0] = running_v[...].astype(BF)

    received(logw_got.at[0 : nch - 1], l_recv)
    logw = logw_got[0]
    for s in range(1, nch):
        logw = logw + logw_got[s]
    mine = (iota(logw.shape, 0) == lax.rem(me, wrows)) & (iota(logw.shape, 1) == 0)
    lw_ref[0] = jnp.sum(jnp.where(mine, logw, 0.0))
    sent_out(logw_got.at[0 : nch - 1], l_send)
    for jp in range(parts):
        sent_out(back_got.at[jp, 0 : n - 1], b_send.at[jp])


def per_device(
    walkers, green_factor, trial, chol, pattern, owner_counts, chol_group, group_weight, aux
):
    n = owner_counts.shape[0]
    cap, nchol, entries = chol.shape
    wall = aux.shape[0]
    assert walkers.shape[0] == 1 and wall == n
    orbitals = walkers.shape[1]
    chunk, part_size, halves = 128, 16, 2
    nch = nchol // halves // chunk
    assert n % nch == 0
    parts = -(-cap // part_size)
    side = orbitals // NBLK
    wrows = wall * nch // n
    dma = pltpu.SemaphoreType.DMA
    vmem = pl.BlockSpec(memory_space=pltpu.VMEM)
    smem = pl.BlockSpec(memory_space=pltpu.SMEM)
    far = pl.BlockSpec(memory_space=pl.ANY)
    advanced, log_weight = pl.pallas_call(
        functools.partial(kernel, n, cap, part_size, halves, chunk),
        out_shape=(
            jax.ShapeDtypeStruct(walkers.shape, BF),
            jax.ShapeDtypeStruct((1,), F32),
        ),
        in_specs=[far, far, far, far, vmem, smem, vmem, smem, far],
        out_specs=(vmem, smem),
        scratch_shapes=[
            pltpu.VMEM(walkers.shape, BF),
            pltpu.VMEM(green_factor.shape, BF),
            pltpu.VMEM(trial.shape, BF),
            pltpu.VMEM(aux.shape, jnp.int32),
            pltpu.VMEM((cap, nchol, entries), BF),
            pltpu.VMEM((entries, side * chunk), BF),
            pltpu.VMEM((orbitals // chunk * NBLK, side * chunk), BF),
            pltpu.VMEM((parts, n, part_size, entries), BF),
            pltpu.VMEM((parts, n, part_size, entries), BF),
            pltpu.VMEM((parts * part_size, wall, entries), BF),
            pltpu.VMEM((wall, nchol), F32),
            pltpu.VMEM((halves, n, wrows, chunk), F32),
            pltpu.VMEM((halves, n, wrows, chunk), F32),
            pltpu.VMEM((halves, wrows, chunk), F32),
            pltpu.VMEM((halves, n, wrows, chunk), F32),
            pltpu.VMEM((wall, nchol), F32),
            pltpu.VMEM((halves, wall, nchol // halves), BF),
            pltpu.VMEM((wrows, chunk), F32),
            pltpu.VMEM((nch, wrows, chunk), F32),
            pltpu.VMEM((cap, wall, entries), F32),
            pltpu.VMEM((parts * part_size, wall, entries), BF),
            pltpu.VMEM((parts, n, part_size, entries), BF),
            pltpu.VMEM((parts, n, part_size, entries), BF),
            pltpu.VMEM((orbitals, orbitals), BF),
            pltpu.VMEM(walkers.shape[1:], BF),
            pltpu.VMEM(walkers.shape[1:], F32),
            dma((4,)),
            dma((parts, halves)),
            dma((parts,)), dma((parts,)),
            dma((halves,)), dma((halves,)),
            dma((halves,)), dma((halves,)),
            dma, dma,
            dma((parts,)), dma((parts,)),
        ],
        compiler_params=pltpu.CompilerParams(
            collective_id=0, has_side_effects=True, vmem_limit_bytes=56 * 2**20
        ),
        cost_estimate=pl.CostEstimate(
            flops=4 * wall * cap * nchol * entries, bytes_accessed=2 * chol.size, transcendentals=0
        ),
    )(
        walkers, green_factor, trial, chol, pattern.reshape(1, -1), owner_counts,
        chol_group.reshape(1, -1), group_weight, aux,
    )
    return advanced, log_weight


def solution(mesh):
    return jax.shard_map(
        per_device,
        mesh=mesh,
        in_specs=(
            P(("groups", "tile"), None, None),
            P(("groups", "tile"), None, None),
            P(),
            P("tile", None, None),
            P(),
            P(),
            P(),
            P(),
            P("groups", None),
        ),
        out_specs=(P(("groups", "tile"), None, None), P(("groups", "tile"))),
        check_vma=False,
    )
```

```python
import functools

import jax
import jax.numpy as jnp
from jax import lax
from jax.experimental import pallas as pl
from jax.experimental.pallas import tpu as pltpu
from jax.sharding import PartitionSpec as P

NBLK = 32
BF = jnp.bfloat16
F32 = jnp.float32
NT_DIMS = (((1,), (1,)), ((), ()))


def quot(x, k):
    if k & (k - 1) == 0:
        return lax.shift_right_logical(x, jnp.int32(k.bit_length() - 1))
    return lax.div(x, jnp.int32(k))


def mod(x, k):
    if k & (k - 1) == 0:
        return lax.bitwise_and(x, jnp.int32(k - 1))
    return lax.rem(x, jnp.int32(k))


def iota(shape, dim):
    return lax.broadcasted_iota(jnp.int32, shape, dim)


def hot(cond):
    return jnp.where(cond, 1.0, 0.0).astype(BF)


def dot(a, b):
    return jnp.dot(a, b, preferred_element_type=F32)


def swap_matrix(outer, inner):
    size = outer * inner
    row = iota((size, size), 0)
    col = iota((size, size), 1)
    return hot(col == mod(row, inner) * outer + quot(row, inner))


def kernel(
    n, cap, part_size, halves, chunk,
    walk_ref, factor_ref, trial_ref, chol_ref, pattern_ref, counts_ref, cgroup_ref, gweight_ref,
    aux_ref,
    adv_ref, lw_ref,
    chol_v, spots, green_v, sent, got, tiles_v, bias_acc, part, part_got, field_own, field_got,
    field_all, fields_v, logw_own, logw_got, pot_acc, pot_v, back, back_got, v_mat, term_v, running_v,
    chol_sem, a_send, a_recv, r_send, r_recv, f_send, f_recv, l_send, l_recv, b_send, b_recv,
):
    me = lax.axis_index("tile")
    orbitals = walk_ref.shape[1]
    nchol, entries = chol_ref.shape[1], chol_ref.shape[2]
    ntile = pattern_ref.shape[1]
    wall = aux_ref.shape[0]
    side = orbitals // NBLK
    group = chunk // side
    ngroup = NBLK // group
    half = nchol // halves
    nch = half // chunk
    wrows = wall * nch // n
    parts = -(-cap // part_size)
    rows = n * part_size
    mine_k = lax.rem(me, nch)
    offsets = sorted(range(1, n), key=lambda off: (abs(off - n // 2), off))
    others = [lax.rem(me + off, n) for off in offsets]

    def send(src, dst, ssem, rsem, dev):
        return pltpu.make_async_remote_copy(
            src_ref=src, dst_ref=dst, send_sem=ssem, recv_sem=rsem,
            device_id={"tile": dev}, device_id_type=pl.DeviceIdType.MESH,
        )

    def received(ref, sem):
        send(ref, ref, sem, sem, others[0]).wait_recv()

    def sent_out(ref, sem):
        send(ref, ref, sem, sem, others[0]).wait_send()

    barrier = pltpu.get_barrier_semaphore()
    for dst in others:
        pl.semaphore_signal(
            barrier, inc=1, device_id={"tile": dst}, device_id_type=pl.DeviceIdType.MESH
        )
    span = [(jp * part_size, min(cap, (jp + 1) * part_size)) for jp in range(parts)]
    chol_copies = {}
    for jp, (j0, j1) in enumerate(span):
        for h in range(halves):
            piece = (pl.ds(j0, j1 - j0), pl.ds(h * half, half), slice(None))
            chol_copies[jp, h] = pltpu.make_async_copy(
                chol_ref.at[piece], chol_v.at[piece], chol_sem.at[jp, h]
            )
            if jp == 0:
                chol_copies[jp, h].start()

    perm = swap_matrix(side, NBLK)
    factor = dot(perm, factor_ref[0]).astype(BF)
    green = lax.dot_general(
        factor, trial_ref[...], NT_DIMS, preferred_element_type=F32
    ).astype(BF)
    for p in range(side):
        for c in range(ngroup):
            green_v[c * NBLK : (c + 1) * NBLK, p * chunk : (p + 1) * chunk] = green[
                p * NBLK : (p + 1) * NBLK, c * chunk : (c + 1) * chunk
            ]
    pat_row = pattern_ref[...]
    pat_col = jnp.transpose(jnp.broadcast_to(pat_row, (128, ntile)))[:, :1]

    def place(pat):
        return quot(mod(pat, NBLK), group) * NBLK + quot(pat, NBLK)

    pick = hot(place(pat_col) == iota((ntile, ngroup * NBLK), 1))
    put = hot(place(pat_row) == iota((ngroup * NBLK, ntile), 0))
    col_mask = hot(mod(pat_col, group) == quot(iota((ntile, chunk), 1), side))
    col_mask = jnp.concatenate([col_mask] * side, axis=1)
    wide_lane = iota((entries, side * chunk), 1)
    spots[...] = hot(
        iota((entries, side * chunk), 0) == quot(wide_lane, chunk) * side + mod(wide_lane, side)
    )
    chosen = dot(pick, green_v[...]).astype(BF) * col_mask
    green_t = lax.dot_general(chosen, spots[...], NT_DIMS, preferred_element_type=F32).astype(BF)

    first = jnp.int32(0)
    lane = iota((1, rows), 1)
    slot = iota((part_size, ntile), 0)
    tile_lane = iota((part_size, ntile), 1)
    lane_tile = [jnp.full((1, rows), -1, jnp.int32) for _ in range(parts)]
    own = [[] for _ in range(parts)]
    for d in range(n):
        held = counts_ref[d]
        for jp in range(parts):
            at = slot + jp * part_size
            own[jp].append(jnp.where((tile_lane == at + first) & (at < held), 1.0, 0.0))
            in_part = lane - d * part_size
            at = in_part + jp * part_size
            live = (in_part >= 0) & (in_part < part_size) & (at < held)
            lane_tile[jp] = jnp.where(live, at + first, lane_tile[jp])
        first = first + held

    for jp in range(parts):
        rows_out = dot(jnp.concatenate(own[jp], axis=0).astype(BF), green_t)
        sent[jp] = rows_out.astype(BF).reshape(n, part_size, entries)
        if jp == 0:
            pl.semaphore_wait(barrier, n - 1)
        for dst in others:
            send(sent.at[jp, dst], got.at[jp, me], a_send.at[jp], a_recv.at[jp], dst).start()
        if jp + 1 < parts:
            for h in range(halves):
                chol_copies[jp + 1, h].start()
        got[jp, me] = sent[jp, me]

    logw_parts = []

    def over_tiles(j0, j1, body, carry):
        step = max(u for u in range(1, 8) if (j1 - j0) % u == 0)

        def several(i, carry):
            for u in range(step):
                carry = body(j0 + i * step + u, carry)
            return carry

        return lax.fori_loop(0, (j1 - j0) // step, several, carry)

    def bias_block(jp, h, g0, size):
        j0, j1 = span[jp]
        start = h * half + g0

        def add(j, total):
            return total + lax.dot_general(
                tiles_v[j], chol_v[j, start : start + size, :], NT_DIMS,
                preferred_element_type=F32,
            )

        total = bias_acc[:, start : start + size] if jp else jnp.zeros((wall, size), F32)
        total = over_tiles(j0, j1, add, total)
        if jp < parts - 1:
            bias_acc[:, start : start + size] = total
            return
        for k in range(size // chunk):
            for wg in range(n // nch):
                part[h, wg * nch + g0 // chunk + k] = total[
                    wg * wrows : (wg + 1) * wrows, k * chunk : (k + 1) * chunk
                ]
        if g0 + size == half:
            for dst in others:
                send(
                    part.at[h, dst], part_got.at[h, me], r_send.at[h], r_recv.at[h], dst
                ).start()
            part_got[h, me] = part[h, me]

    def reduce_bias(h):
        received(part_got.at[h, 0 : n - 1], r_recv.at[h])
        bias = part_got[h, 0]
        for s in range(1, n):
            bias = bias + part_got[h, s]
        drawn = jnp.zeros((wrows, chunk), jnp.int32)
        kind = jnp.zeros((1, chunk), jnp.int32)
        for d in range(n):
            g0 = h * half + (d % nch) * chunk
            w0 = (d // nch) * wrows
            drawn = jnp.where(me == d, aux_ref[w0 : w0 + wrows, g0 : g0 + chunk], drawn)
            kind = jnp.where(me == d, cgroup_ref[:, g0 : g0 + chunk], kind)
        weight = jnp.zeros((1, chunk), F32)
        for k in range(gweight_ref.shape[0]):
            weight = jnp.where(kind == k, gweight_ref[k], weight)
        sampled = drawn.astype(F32) * (1.0 / 262144.0)
        field_own[h] = (weight * (sampled - bias)).astype(BF).astype(F32)
        for dst in others:
            send(
                field_own.at[h], field_got.at[h, me], f_send.at[h], f_recv.at[h], dst
            ).start()
        field_got[h, me] = field_own[h]
        logw_parts.append(
            jnp.sum(sampled * bias - 0.5 * bias * bias, axis=1, keepdims=True)
        )

    def gather_fields(h):
        received(field_got.at[h, 0 : n - 1], f_recv.at[h])
        for s in range(n):
            g0 = h * half + (s % nch) * chunk
            w0 = (s // nch) * wrows
            field_all[w0 : w0 + wrows, g0 : g0 + chunk] = field_got[h, s]
        fields_v[h] = field_all[:, h * half : (h + 1) * half].astype(BF)

    for jp in range(parts):
        received(got.at[jp, 0 : n - 1], a_recv.at[jp])
        j0 = jp * part_size
        tiles_v[j0 : j0 + part_size] = dot(
            swap_matrix(part_size, wall), got[jp].reshape(rows, entries)
        ).astype(BF).reshape(part_size, wall, entries)
        for h in range(halves):
            chol_copies[jp, h].wait()
            if jp == parts - 1 and h > 0:
                bias_block(jp, h, 0, half // 2)
                reduce_bias(h - 1)
                bias_block(jp, h, half // 2, half // 2)
            else:
                bias_block(jp, h, 0, half)

    gather_fields(0)
    for h in range(halves - 1):
        for jp, (j0, j1) in enumerate(span):
            def spread(j, carry):
                new = dot(fields_v[h], chol_v[j, h * half : (h + 1) * half, :])
                pot_acc[j] = new if h == 0 else pot_acc[j] + new
                return carry

            over_tiles(j0, j1, spread, 0)
            if jp == 0 and h == halves - 2:
                reduce_bias(halves - 1)
        gather_fields(h + 1)
    h = halves - 1
    for jp, (j0, j1) in enumerate(span):
        def finish(j, carry):
            pot_v[j] = (
                pot_acc[j] + dot(fields_v[h], chol_v[j, h * half : (h + 1) * half, :])
            ).astype(BF)
            return carry

        over_tiles(j0, j1, finish, 0)
        for j in range(j1, j0 + part_size):
            pot_v[j] = jnp.zeros((wall, entries), BF)
        back[jp] = dot(
            swap_matrix(wall, part_size), pot_v[j0 : j0 + part_size].reshape(rows, entries)
        ).astype(BF).reshape(n, part_size, entries)
        for dst in others:
            send(
                back.at[jp, dst], back_got.at[jp, me], b_send.at[jp], b_recv.at[jp], dst
            ).start()
        back_got[jp, me] = back[jp, me]

    logw = sum(logw_parts[1:], logw_parts[0])
    logw_own[...] = jnp.broadcast_to(logw, logw_own.shape)
    for off in range(1, nch):
        dst = me - mine_k + lax.rem(mine_k + off, nch)
        send(logw_own, logw_got.at[mine_k], l_send, l_recv, dst).start()
    logw_got[mine_k] = logw_own[...]
    unperm = swap_matrix(NBLK, side)
    gather = [hot(iota((ntile, rows), 0) == lane_tile[jp]) for jp in range(parts)]

    for h in range(halves):
        sent_out(part_got.at[h, 0 : n - 1], r_send.at[h])
        sent_out(field_got.at[h, 0 : n - 1], f_send.at[h])
    for jp in range(parts):
        sent_out(got.at[jp, 0 : n - 1], a_send.at[jp])

    pot_t = jnp.zeros((ntile, entries), F32)
    for jp in range(parts):
        received(back_got.at[jp, 0 : n - 1], b_recv.at[jp])
        pot_t = pot_t + dot(gather[jp], back_got[jp].reshape(rows, entries))
    wide = dot(pot_t.astype(BF), spots[...]).astype(BF) * col_mask
    placed = dot(put, wide).astype(BF)
    for p in range(side):
        for c in range(ngroup):
            v_mat[p * NBLK : (p + 1) * NBLK, c * chunk : (c + 1) * chunk] = placed[
                c * NBLK : (c + 1) * NBLK, p * chunk : (p + 1) * chunk
            ]
    v_mat[...] = dot(unperm, v_mat[...]).astype(BF)
    term_v[...] = walk_ref[0]
    running_v[...] = walk_ref[0].astype(F32)

    def taylor(degree, carry):
        term = (dot(v_mat[...], term_v[...]) / degree.astype(F32)).astype(BF)
        term_v[...] = term
        running_v[...] = running_v[...] + term.astype(F32)
        return carry

    lax.fori_loop(1, 5, taylor, 0)
    adv_ref[0] = running_v[...].astype(BF)

    received(logw_got.at[0 : nch - 1], l_recv)
    logw = logw_got[0]
    for s in range(1, nch):
        logw = logw + logw_got[s]
    mine = (iota(logw.shape, 0) == lax.rem(me, wrows)) & (iota(logw.shape, 1) == 0)
    lw_ref[0] = jnp.sum(jnp.where(mine, logw, 0.0))
    sent_out(logw_got.at[0 : nch - 1], l_send)
    for jp in range(parts):
        sent_out(back_got.at[jp, 0 : n - 1], b_send.at[jp])


def per_device(
    walkers, green_factor, trial, chol, pattern, owner_counts, chol_group, group_weight, aux
):
    n = owner_counts.shape[0]
    cap, nchol, entries = chol.shape
    wall = aux.shape[0]
    assert walkers.shape[0] == 1 and wall == n
    orbitals = walkers.shape[1]
    chunk, part_size, halves = 128, 16, 2
    nch = nchol // halves // chunk
    assert n % nch == 0
    parts = -(-cap // part_size)
    side = orbitals // NBLK
    wrows = wall * nch // n
    dma = pltpu.SemaphoreType.DMA
    vmem = pl.BlockSpec(memory_space=pltpu.VMEM)
    smem = pl.BlockSpec(memory_space=pltpu.SMEM)
    advanced, log_weight = pl.pallas_call(
        functools.partial(kernel, n, cap, part_size, halves, chunk),
        out_shape=(
            jax.ShapeDtypeStruct(walkers.shape, BF),
            jax.ShapeDtypeStruct((1,), F32),
        ),
        in_specs=[vmem, vmem, vmem, pl.BlockSpec(memory_space=pl.ANY), vmem, smem, vmem, smem, vmem],
        out_specs=(vmem, smem),
        scratch_shapes=[
            pltpu.VMEM((cap, nchol, entries), BF),
            pltpu.VMEM((entries, side * chunk), BF),
            pltpu.VMEM((orbitals // chunk * NBLK, side * chunk), BF),
            pltpu.VMEM((parts, n, part_size, entries), BF),
            pltpu.VMEM((parts, n, part_size, entries), BF),
            pltpu.VMEM((parts * part_size, wall, entries), BF),
            pltpu.VMEM((wall, nchol), F32),
            pltpu.VMEM((halves, n, wrows, chunk), F32),
            pltpu.VMEM((halves, n, wrows, chunk), F32),
            pltpu.VMEM((halves, wrows, chunk), F32),
            pltpu.VMEM((halves, n, wrows, chunk), F32),
            pltpu.VMEM((wall, nchol), F32),
            pltpu.VMEM((halves, wall, nchol // halves), BF),
            pltpu.VMEM((wrows, chunk), F32),
            pltpu.VMEM((nch, wrows, chunk), F32),
            pltpu.VMEM((cap, wall, entries), F32),
            pltpu.VMEM((parts * part_size, wall, entries), BF),
            pltpu.VMEM((parts, n, part_size, entries), BF),
            pltpu.VMEM((parts, n, part_size, entries), BF),
            pltpu.VMEM((orbitals, orbitals), BF),
            pltpu.VMEM(walkers.shape[1:], BF),
            pltpu.VMEM(walkers.shape[1:], F32),
            dma((parts, halves)),
            dma((parts,)), dma((parts,)),
            dma((halves,)), dma((halves,)),
            dma((halves,)), dma((halves,)),
            dma, dma,
            dma((parts,)), dma((parts,)),
        ],
        compiler_params=pltpu.CompilerParams(
            collective_id=0, has_side_effects=True, vmem_limit_bytes=56 * 2**20
        ),
        cost_estimate=pl.CostEstimate(
            flops=4 * wall * cap * nchol * entries, bytes_accessed=2 * chol.size, transcendentals=0
        ),
    )(
        walkers, green_factor, trial, chol, pattern.reshape(1, -1), owner_counts,
        chol_group.reshape(1, -1), group_weight, aux,
    )
    return advanced, log_weight


def solution(mesh):
    return jax.shard_map(
        per_device,
        mesh=mesh,
        in_specs=(
            P(("groups", "tile"), None, None),
            P(("groups", "tile"), None, None),
            P(),
            P("tile", None, None),
            P(),
            P(),
            P(),
            P(),
            P("groups", None),
        ),
        out_specs=(P(("groups", "tile"), None, None), P(("groups", "tile"))),
        check_vma=False,
    )
```
